256 devices in a mesh: sensor: 8 (over z_lo, x), param: 32 (over z_hi, y, core).
Axes of the slice: x: 4, y: 4, z: 8 (z_hi: 4, z_lo: 2; z = z_hi * 2 + z_lo), core: 2. Of those that a mesh axis runs over, the one named last changes fastest.
Arguments:
- histories: bfloat16 [2048, 6, 256], P(('param', 'sensor')), may hold values from -6 to 6
- kernel: bfloat16 [512, 2048, 256], P('sensor', 'param'), may hold values from -0.015625 to 0.015625
- noise_weight: float32 [512, 256], P('sensor'), may hold values from 0.5 to 8
Outputs:
- hessian_action: float32 [2048, 6, 256], P(('param', 'sensor'))
The draws below stay inside these ranges and needn't reach their ends.
All inputs are finite; a program needn't handle non-finite values.
Results may differ from the reference program's by a relative error of at most 0.0027.
Values may be sent and summed in bfloat16 or wider, within the bound.
A program may use at most 64 MiB of HBM per device.

```python
import math
import jax
import jax.numpy as jnp
from jax import lax

NS = 512
NT = 256
TAPS_BLOCK = 16
NV = 6
NPAR = 2048


def raised(values, key, source, target, shards_of, factor):
    def block_of(axis_at):
        return (jnp.arange(values.shape[axis_at]) // (values.shape[axis_at] // shards_of)).reshape((-1,) + (1,) * (values.ndim - 1 - axis_at))

    first = jax.random.permutation(key, shards_of)[block_of(target)]
    second = (block_of(target) + shards_of // 2) % shards_of
    return jnp.where((block_of(source) == first) | (block_of(source) == second), factor * values, values)


def level_of(stream_key, dims, split, smallest, top_value):
    def one(dim, blocks):
        heights = jax.random.uniform(jax.random.fold_in(jax.random.fold_in(stream_key, 6), dim), (blocks,), jnp.float32, smallest / len(split), top_value / len(split))
        return jnp.repeat(jnp.exp(heights), dims[dim] // blocks).reshape((-1,) + (1,) * (len(dims) - dim - 1))

    level = one(*split[0])
    for cut in split[1:]:
        level = level * one(*cut)
    return level


def bell_draw(key, extent, spread, limit, cuts=(), kind=jnp.bfloat16):
    drawn = spread * jax.random.normal(key, extent, jnp.float32)
    if cuts:
        drawn = drawn * level_of(key, extent, cuts, -0.22, 0.18)
    return jnp.clip(drawn, -limit, limit).astype(kind)


def bell_draw_with(stream_key, dims, scale, limit, split, heavy, kind=jnp.bfloat16):
    array = scale * jax.random.normal(stream_key, dims, jnp.float32)
    if split:
        array = array * level_of(stream_key, dims, split, -0.22, 0.18)
    return jnp.clip(raised(array, jax.random.fold_in(stream_key, 3), *heavy), -limit, limit).astype(kind)


def setup_inputs(seed: int = 0) -> dict:
    streams_of = jax.random.split(jax.random.key(seed), 4)
    histories = bell_draw(streams_of[0], (NPAR, NV, NT), 1.0, 6.0, ((0, 256),))
    kernel = bell_draw_with(streams_of[1], (NS, NPAR, NT), (NPAR * NT) ** -0.5, 0.015625, ((0, 8), (1, 32)), (0, 1, 32, 2.75))
    noise_weight = jnp.clip(jnp.exp(math.log(8.0) - 2.7725887 * jax.random.uniform(streams_of[2], (NS, NT), jnp.float32) ** level_of(streams_of[2], (NS, NT), ((0, 8),), -0.2, 0.2)), 0.5, 8.0)
    return {"histories": histories, "kernel": kernel, "noise_weight": noise_weight}


def reference(histories, kernel, noise_weight):
    length = NT
    hist32 = histories.astype(jnp.float32)
    padded_hist = jnp.pad(hist32, ((0, 0), (0, 0), (length, 0)))

    def forward_step(total, block_index):
        first = block_index * TAPS_BLOCK

        def shifted_one(offset):
            return lax.dynamic_slice_in_dim(padded_hist, length - first - offset, length, 2)

        shifted = jax.vmap(shifted_one)(jnp.arange(TAPS_BLOCK, dtype=jnp.int32))
        taps = lax.dynamic_slice_in_dim(kernel, first, TAPS_BLOCK, 2).astype(jnp.float32)
        term = jnp.einsum('ijk,kjvt->ivt', taps, shifted, precision=lax.Precision.HIGHEST)
        return total + term, None

    blocks = jnp.arange(length // TAPS_BLOCK, dtype=jnp.int32)
    predicted, _ = lax.scan(forward_step, jnp.zeros((NS, NV, length), jnp.float32), blocks)
    weighted = (noise_weight[:, None, :] * predicted).astype(jnp.bfloat16)
    padded_data = jnp.pad(weighted.astype(jnp.float32), ((0, 0), (0, 0), (0, length)))

    def adjoint_step(total, block_index):
        first = block_index * TAPS_BLOCK

        def shifted_one(offset):
            return lax.dynamic_slice_in_dim(padded_data, first + offset, length, 2)

        shifted = jax.vmap(shifted_one)(jnp.arange(TAPS_BLOCK, dtype=jnp.int32))
        taps = lax.dynamic_slice_in_dim(kernel, first, TAPS_BLOCK, 2).astype(jnp.float32)
        term = jnp.einsum('ijk,kivs->jvs', taps, shifted, precision=lax.Precision.HIGHEST)
        return total + term, None

    hessian_action, _ = lax.scan(adjoint_step, jnp.zeros((NPAR, NV, length), jnp.float32), blocks)
    return hessian_action
```

```python
import jax
import jax.numpy as jnp
from jax import lax
from jax.experimental import pallas as pl
from jax.experimental.pallas import tpu as pltpu
from jax.sharding import PartitionSpec as P

F32, BF16 = jnp.float32, jnp.bfloat16
MESH = pl.DeviceIdType.MESH


def lane_of(rows):
    return lax.broadcasted_iota(jnp.int32, (rows, 128), 1)


def spread(xs):
    lane = lane_of(xs[0].shape[0])
    for s in (1, 2, 4):
        low = (lane & s) == 0
        new = list(xs)
        for a in range(8):
            if not a & s:
                new[a] = jnp.where(low, xs[a], pltpu.roll(xs[a | s], s, 1))
                new[a | s] = jnp.where(low, pltpu.roll(xs[a], 128 - s, 1), xs[a | s])
        xs = new
    return xs


def put_taps(a_ref, q, h, g, xs):
    ys = spread(xs)
    col = pl.ds(pl.multiple_of(h * 1024 + g * 128, 128), 128)
    for c in range(8):
        row = pl.multiple_of(c * 32 + 16 * (q % 2), 16)
        a_ref[q // 2, pl.ds(row, 16), col] = ys[c].astype(BF16)


def forward_taps(k_ref, wide_ref, a_ref):
    @pl.loop(0, 64)
    def _(i):
        for h in range(2):
            wide_ref[h, pl.ds(i * 64, 64), :] = k_ref[i, :, 128 * h : 128 * h + 128].astype(F32)

    for h in range(2):

        @pl.loop(0, 32)
        def _(step):
            g, q = step // 4, step % 4
            put_taps(
                a_ref, q, h, g, [wide_ref[h, pl.ds(q * 1024 + 8 * g + j, 16, stride=64), :] for j in range(8)]
            )


def adjoint_taps(k_ref, a_ref, h):
    @pl.loop(0, 32)
    def _(step):
        g, q = step // 4, step % 4
        row = pl.ds(pl.multiple_of(16 * q, 16), 16)
        put_taps(a_ref, q, h, g, [k_ref[8 * g + i, row, 128 * h : 128 * h + 128].astype(F32) for i in range(8)])


def put_shifts(t_ref, g, v, first, second):
    col = pl.ds(v * 128, 128)
    for q in range(8):
        row = pl.multiple_of(g * 128 + 16 * q, 16)
        t_ref[pl.ds(row, 16), col] = jnp.concatenate(first[2 * q : 2 * q + 2], 0).astype(BF16)
        t_ref[pl.ds(1024 + row, 16), col] = jnp.concatenate(second[2 * q : 2 * q + 2], 0).astype(BF16)


def later(lo, hi, s):
    if s == 0:
        return lo, hi
    lane = lane_of(lo.shape[0])
    a, b = pltpu.roll(lo, s, 1), pltpu.roll(hi, s, 1)
    return jnp.where(lane < s, 0.0, a), jnp.where(lane < s, a, b)


def earlier(lo, hi, s):
    if s == 0:
        return lo, hi
    lane = lane_of(lo.shape[0])
    a, b = pltpu.roll(lo, 128 - s, 1), pltpu.roll(hi, 128 - s, 1)
    return jnp.where(lane < 128 - s, a, b), jnp.where(lane < 128 - s, b, 0.0)


def forward_shifts(t_ref, g, v, lo, hi):
    pairs = [later(lo, hi, 8 * l) for l in range(16)]
    put_shifts(t_ref, g, v, [b for _, b in pairs], [a for a, _ in pairs])


def adjoint_shifts(t_ref, g, v, lo, hi):
    pairs = [earlier(lo, hi, 8 * l) for l in range(16)]
    put_shifts(t_ref, g, v, [a for a, _ in pairs], [b for _, b in pairs])


def products(a_ref, half, t_ref, vp, long_ref, short_ref):
    col = pl.ds(pl.multiple_of(vp * 256, 256), 256)
    long_ref[...] = jnp.dot(a_ref[half], t_ref[:, col], preferred_element_type=F32)
    short_ref[...] = jnp.dot(a_ref[half, :, :1024], t_ref[1024:, col], preferred_element_type=F32)


def folded(shift, lo_ref, hi_ref, r, k):
    col = slice(128 * k, 128 * k + 128)
    lo = hi = None
    for c in range(8):
        row = pl.ds(c * 32 + 8 * r, 8)
        a, b = shift(lo_ref[row, col], hi_ref[row, col], c)
        lo, hi = (a, b) if lo is None else (lo + a, hi + b)
    return lo, hi


def body(
    k_hbm, hist_hbm, noise_hbm, out_ref,
    k_ref, hist_ref, noise_ref, wide_ref, a1_ref, a2_ref, t_ref, long_ref, short_ref,
    hb, ybuf, yrecv, ystage, zbuf, zrecv, wall, gf, gmsg, grecv,
    load_sem, h_send, h_recv, c_send, c_recv, y_send, y_recv, z_send, z_recv,
    wz_send, wz_recv, wy_send, wy_recv, wc_send, wc_recv, g_send, g_recv,
):
    ms, mp = lax.axis_index("sensor"), lax.axis_index("param")
    zh, y, core = mp // 8, (mp // 2) % 4, mp % 2

    def sensor_at(s):
        return {"sensor": s, "param": mp}

    def param_at(z_, y_, core_):
        return {"sensor": ms, "param": z_ * 8 + y_ * 2 + core_}

    loads = [
        pltpu.make_async_copy(hist_hbm, hist_ref, load_sem.at[0]),
        pltpu.make_async_copy(k_hbm, k_ref, load_sem.at[1]),
        pltpu.make_async_copy(noise_hbm, noise_ref, load_sem.at[2]),
    ]
    for load in loads:
        load.start()

    barrier = pltpu.get_barrier_semaphore()
    peers = [sensor_at((ms + k) % 8) for k in range(1, 8)]
    peers += [param_at(zh, y, 1 - core)]
    peers += [param_at(zh, (y + k) % 4, core) for k in range(1, 4)]
    peers += [param_at((zh + k) % 4, y, core) for k in range(1, 4)]
    for peer in peers:
        pl.semaphore_signal(barrier, inc=1, device_id=peer, device_id_type=MESH)

    loads[0].wait()
    own = hist_ref[...].astype(F32)
    hb[ms] = jnp.concatenate([own[:, v, :] for v in range(6)], 0).astype(BF16)
    pl.semaphore_wait(barrier, 14)

    def send(src, dst, send_sem, recv_sem, peer):
        copy = pltpu.make_async_remote_copy(
            src_ref=src, dst_ref=dst, send_sem=send_sem, recv_sem=recv_sem, device_id=peer, device_id_type=MESH
        )
        copy.start()
        return copy

    def arrive(dst, recv_sem):
        pltpu.make_async_remote_copy(
            src_ref=dst, dst_ref=dst, send_sem=recv_sem, recv_sem=recv_sem, device_id=sensor_at((ms + 1) % 8),
            device_id_type=MESH,
        ).wait_recv()

    sent = []
    for k in (2, 6, 1, 3, 5, 7, 4):
        sent.append(send(hb.at[ms], hb.at[ms], h_send.at[k], h_recv.at[ms], sensor_at((ms + k) % 8)))

    loads[1].wait()
    forward_taps(k_ref, wide_ref, a1_ref)

    @pl.loop(0, 8)
    def _(k):
        s = (ms + k) % 8

        @pl.when(k > 0)
        def _():
            arrive(hb.at[s], h_recv.at[s])

        block = hb[s].astype(F32)
        for v in range(6):
            forward_shifts(t_ref, s, v, block[8 * v : 8 * v + 8, :128], block[8 * v : 8 * v + 8, 128:])

    for part in range(2):
        half = core if part else 1 - core

        @pl.loop(0, 3)
        def _(vp):
            products(a1_ref, half, t_ref, vp, long_ref, short_ref)
            for r in range(4):
                for k in range(2):
                    lo, hi = folded(later, short_ref, long_ref, r, k)
                    ybuf[part, r, :, pl.ds(pl.multiple_of(256 * vp + 128 * k, 128), 128)] = lo
                    ybuf[part, r, :, pl.ds(pl.multiple_of(768 + 256 * vp + 128 * k, 128), 128)] = hi

        if part == 0:
            sent.append(send(ybuf.at[0], yrecv, c_send, c_recv, param_at(zh, y, 1 - core)))

    arrive(yrecv, c_recv)
    for k in (2, 1, 3):
        to = (y + k) % 4
        ybuf[1, to] = ybuf[1, to] + yrecv[to]
        sent.append(send(ybuf.at[1, to], ystage.at[y], y_send.at[k], y_recv.at[y], param_at(zh, to, core)))

    adjoint_taps(k_ref, a2_ref, 0)

    total = ybuf[1, y] + yrecv[y]
    for k in (1, 3, 2):
        at = (y + k) % 4
        arrive(ystage.at[at], y_recv.at[at])
        total = total + ystage[at]
    for z in range(4):
        zbuf[z] = total[:, 384 * z : 384 * z + 384]
    for k in (2, 1, 3):
        to = (zh + k) % 4
        sent.append(send(zbuf.at[to], zrecv.at[zh], z_send.at[k], z_recv.at[zh], param_at(to, y, core)))
    loads[2].wait()
    group = core * 4 + y
    noise = noise_ref[pl.ds(pl.multiple_of(8 * group, 8), 8), pl.ds(pl.multiple_of(128 * (zh // 2), 128), 128)]
    piece = zbuf[zh]
    for k in (1, 3, 2):
        at = (zh + k) % 4
        arrive(zrecv.at[at], z_recv.at[at])
        piece = piece + zrecv[at]
    tiles = [piece[:, 128 * k : 128 * k + 128] * noise for k in range(3)]
    tiles.append(jnp.zeros_like(noise))
    wall[group * 4 + zh] = jnp.concatenate(
        [jnp.concatenate(tiles[:2], 1), jnp.concatenate(tiles[2:], 1)], 0
    ).astype(BF16)
    for k in (2, 1, 3):
        here = group * 4 + zh
        sent.append(
            send(wall.at[here], wall.at[here], wz_send.at[k], wz_recv.at[zh], param_at((zh + k) % 4, y, core))
        )

    adjoint_taps(k_ref, a2_ref, 1)

    for k in (1, 3, 2):
        at = (zh + k) % 4
        arrive(wall.at[group * 4 + at], wz_recv.at[at])
    block = wall.at[pl.ds(group * 4, 4)]
    for k in (2, 1, 3):
        sent.append(send(block, block, wy_send.at[k], wy_recv.at[y], param_at(zh, (y + k) % 4, core)))
    sent.append(send(block, block, wc_send.at[y], wc_recv.at[y], param_at(zh, y, 1 - core)))

    def weighted_shifts(g):
        pieces = [wall[g * 4 + z].astype(F32) for z in range(4)]
        for v in range(6):
            row, col = 8 * (v % 3 // 2), 128 * (v % 3 % 2)
            lo, hi = [pieces[z][row : row + 8, col : col + 128] for z in (v // 3, 2 + v // 3)]
            adjoint_shifts(t_ref, g, v, lo, hi)

    @pl.loop(0, 8)
    def _(step):
        at = (y + step) % 4
        mine = step < 4
        g = jnp.where(mine, core, 1 - core) * 4 + at
        here = wall.at[pl.ds(g * 4, 4)]

        @pl.when((step > 0) & mine)
        def _():
            arrive(here, wy_recv.at[at])
            send(here, here, wc_send.at[at], wc_recv.at[at], param_at(zh, y, 1 - core))

        @pl.when(step >= 4)
        def _():
            arrive(here, wc_recv.at[at])

        weighted_shifts(g)

    for part in range(2):
        half = ms // 4 if part else 1 - ms // 4

        @pl.loop(0, 3)
        def _(vp):
            products(a2_ref, half, t_ref, vp, long_ref, short_ref)
            for r in range(4):
                for k in range(2):
                    lo, hi = folded(earlier, long_ref, short_ref, r, k)
                    gf[part, r, :, pl.ds(pl.multiple_of(256 * vp + 128 * k, 128), 128)] = jnp.concatenate([lo, hi], 0)

        for k in (2, 1, 3, 0):
            to = (ms + k) % 4
            if part and k == 0:
                continue
            slot = half * 4 + to
            gmsg[slot] = gf[part, to].astype(BF16)
            sent.append(
                send(gmsg.at[slot], grecv.at[ms], g_send.at[4 * part + k], g_recv.at[ms], sensor_at(slot))
            )

    total = gf[1, ms % 4]
    for k in range(1, 8):
        at = (ms + k) % 8
        arrive(grecv.at[at], g_recv.at[at])
        total = total + grecv[at].astype(F32)
    for v in range(6):
        for t in range(2):
            out_ref[:, v, 128 * t : 128 * t + 128] = total[8 * t : 8 * t + 8, 128 * v : 128 * v + 128]

    for copy in sent:
        copy.wait_send()
    for k in range(1, 4):
        at = (y + k) % 4
        here = wall.at[pl.ds((core * 4 + at) * 4, 4)]
        pltpu.make_async_remote_copy(
            src_ref=here, dst_ref=here, send_sem=wc_send.at[at], recv_sem=wc_recv.at[at],
            device_id=param_at(zh, y, 1 - core), device_id_type=MESH,
        ).wait_send()


def shards(histories, kernel, noise_weight):
    V, S = pltpu.VMEM, pltpu.SemaphoreType.DMA
    return pl.pallas_call(
        body,
        out_shape=jax.ShapeDtypeStruct((8, 6, 256), F32),
        in_specs=[pl.BlockSpec(memory_space=pl.ANY)] * 3,
        out_specs=pl.BlockSpec(memory_space=pltpu.VMEM),
        scratch_shapes=[
            V((64, 64, 256), BF16), V((8, 6, 256), BF16), V((64, 256), F32), V((2, 4096, 128), F32),
            V((2, 256, 2048), BF16), V((2, 256, 2048), BF16), V((2048, 768), BF16), V((256, 256), F32),
            V((256, 256), F32),
            V((8, 48, 256), BF16), V((2, 4, 8, 1536), F32), V((4, 8, 1536), F32), V((4, 8, 1536), F32),
            V((4, 8, 384), F32), V((4, 8, 384), F32), V((32, 16, 256), BF16), V((2, 4, 16, 768), F32),
            V((8, 16, 768), BF16), V((8, 16, 768), BF16),
            S((3,)), S((8,)), S((8,)), S(()), S(()), S((4,)), S((4,)), S((4,)), S((4,)),
            S((4,)), S((4,)), S((4,)), S((4,)), S((4,)), S((4,)), S((8,)), S((8,)),
        ],
        compiler_params=pltpu.CompilerParams(
            collective_id=0, has_side_effects=True, vmem_limit_bytes=48 * 2**20
        ),
        cost_estimate=pl.CostEstimate(flops=4831838208, bytes_accessed=2300000, transcendentals=0),
        name="hessian",
    )(kernel, histories, noise_weight)


def solution(mesh):
    in_specs = (P(("param", "sensor"), None, None), P("sensor", "param", None), P("sensor", None))
    out_specs = P(("param", "sensor"), None, None)
    return jax.shard_map(shards, mesh=mesh, in_specs=in_specs, out_specs=out_specs, check_vma=False)
```

```python
import jax
import jax.numpy as jnp
from jax import lax
from jax.experimental import pallas as pl
from jax.experimental.pallas import tpu as pltpu
from jax.sharding import PartitionSpec as P

F32, BF16 = jnp.float32, jnp.bfloat16
MESH = pl.DeviceIdType.MESH


def lane_of(rows):
    return lax.broadcasted_iota(jnp.int32, (rows, 128), 1)


def fill_order(order_ref):
    row, col = [lax.broadcasted_iota(jnp.int32, (128, 1024), d) for d in (0, 1)]
    low = row & 7
    target = low * 128 + (row - low)

    @pl.loop(0, 8)
    def _(j):
        here = jnp.where(col == target + j, 1.0, 0.0).astype(BF16)
        order_ref[pl.ds(pl.multiple_of(j * 128, 128), 128), :] = here


def put_taps(x, order_ref, a_ref, h, n):
    ys = jnp.dot(x, order_ref[:, pl.ds(pl.multiple_of(n * 256, 256), 256)], preferred_element_type=F32)
    for half in range(2):
        for g in range(8):
            for c in range(2):
                part = ys[64 * g + 32 * half : 64 * g + 32 * half + 32, 128 * c : 128 * c + 128]
                row = pl.ds(pl.multiple_of((2 * n + c) * 32, 32), 32)
                col = pl.ds(pl.multiple_of(h * 1024 + g * 128, 128), 128)
                a_ref[half, row, col] = part.astype(BF16)


def forward_taps(k_ref, wide_ref, x_ref, order_ref, a_ref):
    @pl.loop(0, 32)
    def _(step):
        for u in range(2):
            i = 2 * step + u
            for h in range(2):
                wide_ref[h, pl.ds(pl.multiple_of(i * 72, 8), 64), :] = k_ref[i, :, 128 * h : 128 * h + 128].astype(F32)

    for h in range(2):

        @pl.loop(0, 8)
        def _(g):
            row = pl.ds(pl.multiple_of(64 * g, 64), 64)
            for j in range(8):
                x_ref[h, row, 128 * j : 128 * j + 128] = wide_ref[h, pl.ds(8 * g + j, 64, stride=72), :].astype(BF16)

    @pl.loop(0, 8)
    def _(step):
        put_taps(x_ref[step // 4], order_ref, a_ref, step // 4, step % 4)


def adjoint_taps(k_ref, order_ref, a_ref, h):
    @pl.loop(0, 4)
    def _(n):
        x = [
            jnp.concatenate([k_ref[8 * g + i, :, 128 * h : 128 * h + 128] for g in range(8)], 0) for i in range(8)
        ]
        put_taps(jnp.concatenate(x, 1), order_ref, a_ref, h, n)


def put_shifts(t_ref, g, v, first, second):
    col = pl.ds(v * 128, 128)
    for q in range(8):
        row = pl.multiple_of(g * 128 + 16 * q, 16)
        t_ref[pl.ds(row, 16), col] = jnp.concatenate(first[2 * q : 2 * q + 2], 0).astype(BF16)
        t_ref[pl.ds(1024 + row, 16), col] = jnp.concatenate(second[2 * q : 2 * q + 2], 0).astype(BF16)


def later(lo, hi, s):
    if s == 0:
        return lo, hi
    lane = lane_of(lo.shape[0])
    a, b = pltpu.roll(lo, s, 1), pltpu.roll(hi, s, 1)
    return jnp.where(lane < s, 0.0, a), jnp.where(lane < s, a, b)


def earlier(lo, hi, s):
    if s == 0:
        return lo, hi
    lane = lane_of(lo.shape[0])
    a, b = pltpu.roll(lo, 128 - s, 1), pltpu.roll(hi, 128 - s, 1)
    return jnp.where(lane < 128 - s, a, b), jnp.where(lane < 128 - s, b, 0.0)


def forward_shifts(t_ref, g, v, lo, hi):
    pairs = [later(lo, hi, 8 * l) for l in range(16)]
    put_shifts(t_ref, g, v, [b for _, b in pairs], [a for a, _ in pairs])


def adjoint_shifts(t_ref, g, v, lo, hi):
    pairs = [earlier(lo, hi, 8 * l) for l in range(16)]
    put_shifts(t_ref, g, v, [a for a, _ in pairs], [b for _, b in pairs])


def products(a_ref, half, t_ref, vp, long_ref, short_ref):
    col = pl.ds(pl.multiple_of(vp * 256, 256), 256)
    long_ref[...] = jnp.dot(a_ref[half], t_ref[:, col], preferred_element_type=F32)
    short_ref[...] = jnp.dot(a_ref[half, :, :1024], t_ref[1024:, col], preferred_element_type=F32)


def folded(shift, lo_ref, hi_ref, r, k):
    col = slice(128 * k, 128 * k + 128)
    lo = hi = None
    for c in range(8):
        row = pl.ds(c * 32 + 8 * r, 8)
        a, b = shift(lo_ref[row, col], hi_ref[row, col], c)
        lo, hi = (a, b) if lo is None else (lo + a, hi + b)
    return lo, hi


def body(
    k_hbm, hist_hbm, noise_hbm, out_ref,
    k_ref, noise_ref, wide_ref, x_ref, order_ref, a1_ref, a2_ref, t_ref, long_ref, short_ref,
    hb, ybuf, yrecv, ystage, zbuf, zrecv, wall, gf, gmsg, grecv,
    load_sem, h_send, h_recv, c_send, c_recv, y_send, y_recv, z_send, z_recv,
    wz_send, wz_recv, wy_send, wy_recv, wc_send, wc_recv, g_send, g_recv,
):
    ms, mp = lax.axis_index("sensor"), lax.axis_index("param")
    zh, y, core = mp // 8, (mp // 2) % 4, mp % 2

    def sensor_at(s):
        return {"sensor": s, "param": mp}

    def param_at(z_, y_, core_):
        return {"sensor": ms, "param": z_ * 8 + y_ * 2 + core_}

    loads = [
        pltpu.make_async_copy(hist_hbm, hb.at[ms], load_sem.at[0]),
        pltpu.make_async_copy(k_hbm, k_ref, load_sem.at[1]),
        pltpu.make_async_copy(noise_hbm, noise_ref, load_sem.at[2]),
    ]
    for load in loads:
        load.start()

    barrier = pltpu.get_barrier_semaphore()
    peers = [sensor_at((ms + k) % 8) for k in range(1, 8)]
    peers += [param_at(zh, y, 1 - core)]
    peers += [param_at(zh, (y + k) % 4, core) for k in range(1, 4)]
    peers += [param_at((zh + k) % 4, y, core) for k in range(1, 4)]
    for peer in peers:
        pl.semaphore_signal(barrier, inc=1, device_id=peer, device_id_type=MESH)

    fill_order(order_ref)
    loads[0].wait()
    pl.semaphore_wait(barrier, 14)

    def send(src, dst, send_sem, recv_sem, peer):
        copy = pltpu.make_async_remote_copy(
            src_ref=src, dst_ref=dst, send_sem=send_sem, recv_sem=recv_sem, device_id=peer, device_id_type=MESH
        )
        copy.start()
        return copy

    def arrive(dst, recv_sem):
        pltpu.make_async_remote_copy(
            src_ref=dst, dst_ref=dst, send_sem=recv_sem, recv_sem=recv_sem, device_id=sensor_at((ms + 1) % 8),
            device_id_type=MESH,
        ).wait_recv()

    sent = []
    for k in (2, 6, 1, 3, 5, 7, 4):
        sent.append(send(hb.at[ms], hb.at[ms], h_send.at[k], h_recv.at[ms], sensor_at((ms + k) % 8)))

    loads[1].wait()
    forward_taps(k_ref, wide_ref, x_ref, order_ref, a1_ref)

    @pl.loop(0, 8)
    def _(k):
        s = (ms + k) % 8

        @pl.when(k > 0)
        def _():
            arrive(hb.at[s], h_recv.at[s])

        block = hb[s].astype(F32)
        for v in range(6):
            forward_shifts(t_ref, s, v, block[8 * v : 8 * v + 8, :128], block[8 * v : 8 * v + 8, 128:])

    for part in range(2):
        half = core if part else 1 - core

        @pl.loop(0, 3)
        def _(vp):
            products(a1_ref, half, t_ref, vp, long_ref, short_ref)
            for r in range(4):
                for k in range(2):
                    lo, hi = folded(later, short_ref, long_ref, r, k)
                    ybuf[part, r, :, pl.ds(pl.multiple_of(256 * vp + 128 * k, 128), 128)] = lo
                    ybuf[part, r, :, pl.ds(pl.multiple_of(768 + 256 * vp + 128 * k, 128), 128)] = hi

        if part == 0:
            sent.append(send(ybuf.at[0], yrecv, c_send, c_recv, param_at(zh, y, 1 - core)))

    arrive(yrecv, c_recv)
    for k in (2, 1, 3):
        to = (y + k) % 4
        ybuf[1, to] = ybuf[1, to] + yrecv[to]
        sent.append(send(ybuf.at[1, to], ystage.at[y], y_send.at[k], y_recv.at[y], param_at(zh, to, core)))

    adjoint_taps(k_ref, order_ref, a2_ref, 0)

    total = ybuf[1, y] + yrecv[y]
    for k in (1, 3, 2):
        at = (y + k) % 4
        arrive(ystage.at[at], y_recv.at[at])
        total = total + ystage[at]
    for z in range(4):
        zbuf[z] = total[:, 384 * z : 384 * z + 384]
    for k in (2, 1, 3):
        to = (zh + k) % 4
        sent.append(send(zbuf.at[to], zrecv.at[zh], z_send.at[k], z_recv.at[zh], param_at(to, y, core)))
    loads[2].wait()
    group = core * 4 + y
    noise = noise_ref[pl.ds(pl.multiple_of(8 * group, 8), 8), pl.ds(pl.multiple_of(128 * (zh // 2), 128), 128)]
    piece = zbuf[zh]
    for k in (1, 3, 2):
        at = (zh + k) % 4
        arrive(zrecv.at[at], z_recv.at[at])
        piece = piece + zrecv[at]
    tiles = [piece[:, 128 * k : 128 * k + 128] * noise for k in range(3)]
    tiles.append(jnp.zeros_like(noise))
    wall[group * 4 + zh] = jnp.concatenate(
        [jnp.concatenate(tiles[:2], 1), jnp.concatenate(tiles[2:], 1)], 0
    ).astype(BF16)
    for k in (2, 1, 3):
        here = group * 4 + zh
        sent.append(
            send(wall.at[here], wall.at[here], wz_send.at[k], wz_recv.at[zh], param_at((zh + k) % 4, y, core))
        )

    adjoint_taps(k_ref, order_ref, a2_ref, 1)

    for k in (1, 3, 2):
        at = (zh + k) % 4
        arrive(wall.at[group * 4 + at], wz_recv.at[at])
    block = wall.at[pl.ds(group * 4, 4)]
    for k in (2, 1, 3):
        sent.append(send(block, block, wy_send.at[k], wy_recv.at[y], param_at(zh, (y + k) % 4, core)))
    sent.append(send(block, block, wc_send.at[y], wc_recv.at[y], param_at(zh, y, 1 - core)))

    def weighted_shifts(g):
        pieces = [wall[g * 4 + z].astype(F32) for z in range(4)]
        for v in range(6):
            row, col = 8 * (v % 3 // 2), 128 * (v % 3 % 2)
            lo, hi = [pieces[z][row : row + 8, col : col + 128] for z in (v // 3, 2 + v // 3)]
            adjoint_shifts(t_ref, g, v, lo, hi)

    @pl.loop(0, 8)
    def _(step):
        at = (y + step) % 4
        mine = step < 4
        g = jnp.where(mine, core, 1 - core) * 4 + at
        here = wall.at[pl.ds(g * 4, 4)]

        @pl.when((step > 0) & mine)
        def _():
            arrive(here, wy_recv.at[at])
            send(here, here, wc_send.at[at], wc_recv.at[at], param_at(zh, y, 1 - core))

        @pl.when(step >= 4)
        def _():
            arrive(here, wc_recv.at[at])

        weighted_shifts(g)

    for part in range(2):
        half = ms // 4 if part else 1 - ms // 4

        @pl.loop(0, 3)
        def _(vp):
            products(a2_ref, half, t_ref, vp, long_ref, short_ref)
            for r in range(4):
                for k in range(2):
                    lo, hi = folded(earlier, long_ref, short_ref, r, k)
                    gf[part, r, :, pl.ds(pl.multiple_of(256 * vp + 128 * k, 128), 128)] = jnp.concatenate([lo, hi], 0)

        for k in (2, 1, 3, 0):
            to = (ms + k) % 4
            if part and k == 0:
                continue
            slot = half * 4 + to
            gmsg[slot] = gf[part, to].astype(BF16)
            sent.append(
                send(gmsg.at[slot], grecv.at[ms], g_send.at[4 * part + k], g_recv.at[ms], sensor_at(slot))
            )

    total = gf[1, ms % 4]
    for k in range(1, 8):
        at = (ms + k) % 8
        arrive(grecv.at[at], g_recv.at[at])
        total = total + grecv[at].astype(F32)
    for v in range(6):
        for t in range(2):
            out_ref[8 * v : 8 * v + 8, 128 * t : 128 * t + 128] = total[8 * t : 8 * t + 8, 128 * v : 128 * v + 128]

    for copy in sent:
        copy.wait_send()
    for k in range(1, 4):
        at = (y + k) % 4
        here = wall.at[pl.ds((core * 4 + at) * 4, 4)]
        pltpu.make_async_remote_copy(
            src_ref=here, dst_ref=here, send_sem=wc_send.at[at], recv_sem=wc_recv.at[at],
            device_id=param_at(zh, y, 1 - core), device_id_type=MESH,
        ).wait_send()


def shards(histories, kernel, noise_weight):
    V, S = pltpu.VMEM, pltpu.SemaphoreType.DMA
    out = pl.pallas_call(
        body,
        out_shape=jax.ShapeDtypeStruct((48, 256), F32),
        in_specs=[pl.BlockSpec(memory_space=pltpu.HBM)] * 3,
        out_specs=pl.BlockSpec(memory_space=pltpu.VMEM),
        scratch_shapes=[
            V((64, 64, 256), BF16), V((64, 256), F32), V((2, 4608, 128), F32), V((2, 512, 1024), BF16), V((1024, 1024), BF16),
            V((2, 256, 2048), BF16), V((2, 256, 2048), BF16), V((2048, 768), BF16), V((256, 256), F32),
            V((256, 256), F32),
            V((8, 48, 256), BF16), V((2, 4, 8, 1536), F32), V((4, 8, 1536), F32), V((4, 8, 1536), F32),
            V((4, 8, 384), F32), V((4, 8, 384), F32), V((32, 16, 256), BF16), V((2, 4, 16, 768), F32),
            V((8, 16, 768), BF16), V((8, 16, 768), BF16),
            S((3,)), S((8,)), S((8,)), S(()), S(()), S((4,)), S((4,)), S((4,)), S((4,)),
            S((4,)), S((4,)), S((4,)), S((4,)), S((4,)), S((4,)), S((8,)), S((8,)),
        ],
        compiler_params=pltpu.CompilerParams(
            collective_id=0, has_side_effects=True, vmem_limit_bytes=60 * 2**20
        ),
        cost_estimate=pl.CostEstimate(flops=4831838208, bytes_accessed=2300000, transcendentals=0),
        name="hessian",
    )(kernel, histories.transpose(1, 0, 2).reshape(48, 256), noise_weight)
    return out.reshape(6, 8, 256).transpose(1, 0, 2)


def solution(mesh):
    in_specs = (P(("param", "sensor"), None, None), P("sensor", "param", None), P("sensor", None))
    out_specs = P(("param", "sensor"), None, None)
    return jax.shard_map(shards, mesh=mesh, in_specs=in_specs, out_specs=out_specs, check_vma=False)
```

```python
import jax
import jax.numpy as jnp
from jax import lax
from jax.experimental import pallas as pl
from jax.experimental.pallas import tpu as pltpu
from jax.sharding import PartitionSpec as P

F32, BF16 = jnp.float32, jnp.bfloat16
MESH = pl.DeviceIdType.MESH


def lane_of(rows):
    return lax.broadcasted_iota(jnp.int32, (rows, 128), 1)


def fill_order(order_ref):
    row, col = [lax.broadcasted_iota(jnp.int32, (128, 1024), d) for d in (0, 1)]
    low = row & 7
    target = low * 128 + (row - low)

    @pl.loop(0, 8)
    def _(j):
        here = jnp.where(col == target + j, 1.0, 0.0).astype(BF16)
        order_ref[pl.ds(pl.multiple_of(j * 128, 128), 128), :] = here


def reordered(x, order_ref, n):
    return jnp.dot(x, order_ref[:, pl.ds(pl.multiple_of(n * 256, 256), 256)], preferred_element_type=F32)


def forward_taps(k_ref, wide_ref, x_ref, order_ref, a_ref):
    for h in range(2):

        @pl.loop(0, 8)
        def _(g):
            row = pl.ds(pl.multiple_of(64 * g, 64), 64)
            for j in range(8):
                x_ref[h, row, 128 * j : 128 * j + 128] = wide_ref[h, pl.ds(8 * g + j, 64, stride=72), :].astype(BF16)

    @pl.loop(0, 8)
    def _(step):
        h, n = step // 4, step % 4
        ys = reordered(x_ref[h], order_ref, n)
        for z in range(4):
            for g in range(8):
                for c in range(2):
                    first = 64 * g + 8 * z
                    part = [ys[r : r + 8, 128 * c : 128 * c + 128] for r in (first, first + 32)]
                    row = pl.ds(pl.multiple_of((2 * n + c) * 16, 16), 16)
                    col = pl.ds(pl.multiple_of(h * 1024 + g * 128, 128), 128)
                    a_ref[z, row, col] = jnp.concatenate(part, 0).astype(BF16)


def adjoint_taps(k_ref, order_ref, a_ref, h):
    @pl.loop(0, 4)
    def _(n):
        x = [
            jnp.concatenate([k_ref[8 * g + i, :, 128 * h : 128 * h + 128] for g in range(8)], 0) for i in range(8)
        ]
        ys = reordered(jnp.concatenate(x, 1), order_ref, n)
        for to in range(2):
            for g in range(8):
                for c in range(2):
                    first = 64 * g + 32 * to
                    row = pl.ds(pl.multiple_of(256 * to + (2 * n + c) * 32, 32), 32)
                    a_ref[g % 4, row, 256 * h + 128 * (g // 4) : 256 * h + 128 * (g // 4) + 128] = ys[
                        first : first + 32, 128 * c : 128 * c + 128
                    ].astype(BF16)


def put_shifts(t_ref, rows, v, series):
    col = pl.ds(v * 128, 128)
    for start, shifted in zip(rows, series):
        for q in range(8):
            row = pl.multiple_of(start + 16 * q, 16)
            t_ref[pl.ds(row, 16), col] = jnp.concatenate(shifted[2 * q : 2 * q + 2], 0).astype(BF16)


def later(lo, hi, s):
    if s == 0:
        return lo, hi
    lane = lane_of(lo.shape[0])
    a, b = pltpu.roll(lo, s, 1), pltpu.roll(hi, s, 1)
    return jnp.where(lane < s, 0.0, a), jnp.where(lane < s, a, b)


def earlier(lo, hi, s):
    if s == 0:
        return lo, hi
    lane = lane_of(lo.shape[0])
    a, b = pltpu.roll(lo, 128 - s, 1), pltpu.roll(hi, 128 - s, 1)
    return jnp.where(lane < 128 - s, a, b), jnp.where(lane < 128 - s, b, 0.0)


def forward_shifts(t_ref, g, v, lo, hi):
    pairs = [later(lo, hi, 8 * l) for l in range(16)]
    put_shifts(t_ref, (1024 + g * 128, g * 128), v, zip(*pairs))


def adjoint_shifts(t_ref, half, v, lo, hi):
    pairs = [earlier(lo, hi, 8 * l) for l in range(16)]
    put_shifts(t_ref, (half * 128, 256 + half * 128), v, zip(*pairs))


def folded(shift, lo_ref, hi_ref, start, stride, v):
    col = slice(128 * v, 128 * v + 128)
    lo = hi = None
    for c in range(8):
        row = pl.ds(start + stride * c, 8)
        a, b = shift(lo_ref[row, col], hi_ref[row, col], c)
        lo, hi = (a, b) if lo is None else (lo + a, hi + b)
    return lo, hi


def body(
    k_hbm, hist_hbm, noise_hbm, out_ref,
    k_ref, noise_ref, wide_ref, x_ref, order_ref, a1_ref, a2_ref, t1_ref, long_ref, short_ref, t2_ref, q0_ref, q1_ref,
    hb, ybuf, yrecv, zrecv, wall, gf, gmsg, grecv,
    load_sem, h_send, h_recv, c_send, c_recv, z_send, z_recv, w_send, w_recv, wc_send, wc_recv, g_send, g_recv,
):
    ms, mp = lax.axis_index("sensor"), lax.axis_index("param")
    zh, y, core = mp // 8, (mp // 2) % 4, mp % 2

    def sensor_at(s):
        return {"sensor": s, "param": mp}

    def param_at(z_, y_, core_):
        return {"sensor": ms, "param": z_ * 8 + y_ * 2 + core_}

    partner = param_at(zh, y, 1 - core)

    pltpu.make_async_copy(hist_hbm, hb.at[ms], load_sem.at[0]).start()
    k_loads = []
    for part in range(4):
        rows = pl.ds(16 * part, 16)
        k_loads.append(pltpu.make_async_copy(k_hbm.at[rows], k_ref.at[rows], load_sem.at[2 + part]))
        k_loads[-1].start()
    pltpu.make_async_copy(noise_hbm, noise_ref, load_sem.at[1]).start()

    barrier = pltpu.get_barrier_semaphore()
    peers = [sensor_at((ms + k) % 8) for k in range(1, 8)]
    peers += [partner]
    peers += [param_at((zh + dz) % 4, (y + dy) % 4, core) for dz in range(4) for dy in range(4) if dz or dy]
    for peer in peers:
        pl.semaphore_signal(barrier, inc=1, device_id=peer, device_id_type=MESH)

    fill_order(order_ref)
    pltpu.make_async_copy(hist_hbm, hb.at[ms], load_sem.at[0]).wait()
    pl.semaphore_wait(barrier, len(peers))

    def send(src, dst, send_sem, recv_sem, peer):
        copy = pltpu.make_async_remote_copy(
            src_ref=src, dst_ref=dst, send_sem=send_sem, recv_sem=recv_sem, device_id=peer, device_id_type=MESH
        )
        copy.start()
        return copy

    def arrive(dst, recv_sem):
        pltpu.make_async_remote_copy(
            src_ref=dst, dst_ref=dst, send_sem=recv_sem, recv_sem=recv_sem, device_id=partner, device_id_type=MESH
        ).wait_recv()

    def sent_off(src, send_sem):
        pltpu.make_async_remote_copy(
            src_ref=src, dst_ref=src, send_sem=send_sem, recv_sem=send_sem, device_id=partner, device_id_type=MESH
        ).wait_send()

    sent = []
    for k in (2, 6, 1, 3, 5, 7, 4):
        sent.append(send(hb.at[ms], hb.at[ms], h_send.at[k], h_recv.at[ms], sensor_at((ms + k) % 8)))

    for part in range(4):
        k_loads[part].wait()

        @pl.loop(8 * part, 8 * part + 8)
        def _(step):
            for u in range(2):
                i = 2 * step + u
                for h in range(2):
                    wide_ref[h, pl.ds(pl.multiple_of(i * 72, 8), 64), :] = k_ref[i, :, 128 * h : 128 * h + 128].astype(F32)

    forward_taps(k_ref, wide_ref, x_ref, order_ref, a1_ref)

    @pl.loop(0, 8)
    def _(k):
        s = (ms + k) % 8

        @pl.when(k > 0)
        def _():
            arrive(hb.at[s], h_recv.at[s])

        block = hb[s].astype(F32)
        for v in range(6):
            forward_shifts(t1_ref, s, v, block[8 * v : 8 * v + 8, :128], block[8 * v : 8 * v + 8, 128:])

    def z_of(b):
        return (zh + jnp.where(b == 0, 2, jnp.where(b == 1, 1, jnp.where(b == 2, 3, 0)))) % 4

    def pass_on(b, dys):
        arrive(yrecv.at[b], c_recv.at[b])
        for dy in dys:
            to = (y + dy) % 4
            ybuf[b, 1, to] = ybuf[b, 1, to] + yrecv[b, to]
            send(
                ybuf.at[b, 1, to], zrecv.at[zh * 4 + y], z_send.at[b, dy], z_recv.at[zh * 4 + y],
                param_at(z_of(b), to, core),
            )

    @pl.loop(0, 4)
    def _(b):
        z = z_of(b)
        long_ref[...] = jnp.dot(a1_ref[z], t1_ref[...], preferred_element_type=F32)
        short_ref[...] = jnp.dot(a1_ref[z, :, :1024], t1_ref[1024:, :], preferred_element_type=F32)
        for half in range(2):
            mine = (half + core + 1) % 2
            for v in range(6):
                lo, hi = folded(later, short_ref, long_ref, 8 * half, 16, v)
                col = slice(128 * (v % 3), 128 * (v % 3) + 128)
                ybuf[b, mine, v // 3, :, col] = lo
                ybuf[b, mine, 2 + v // 3, :, col] = hi
        send(ybuf.at[b, 0], yrecv.at[b], c_send.at[b], c_recv.at[b], partner)

        @pl.when(b > 0)
        def _():
            pass_on(b - 1, (2, 1, 3, 0))

    pass_on(3, (2, 1, 3))

    adjoint_taps(k_ref, order_ref, a2_ref, 0)

    piece = ybuf[3, 1, y] + yrecv[3, y]
    for dz in (2, 1, 3, 0):
        for dy in range(4):
            if dz or dy:
                at = ((zh + dz) % 4) * 4 + (y + dy) % 4
                arrive(zrecv.at[at], z_recv.at[at])
                piece = piece + zrecv[at]

    pltpu.make_async_copy(noise_hbm, noise_ref, load_sem.at[1]).wait()
    group = core * 4 + zh
    noise = noise_ref[pl.ds(pl.multiple_of(8 * group, 8), 8), pl.ds(pl.multiple_of(128 * (y // 2), 128), 128)]
    tiles = [piece[:, 128 * k : 128 * k + 128] * noise for k in range(3)]
    tiles.append(jnp.zeros_like(noise))
    here = group * 4 + y
    wall[here] = jnp.concatenate(
        [jnp.concatenate(tiles[:2], 1), jnp.concatenate(tiles[2:], 1)], 0
    ).astype(BF16)
    for dz in (2, 1, 3, 0):
        for dy in (2, 1, 3, 0):
            if dz or dy:
                peer = param_at((zh + dz) % 4, (y + dy) % 4, core)
                sent.append(send(wall.at[here], wall.at[here], w_send.at[dz * 4 + dy], w_recv.at[zh * 4 + y], peer))

    adjoint_taps(k_ref, order_ref, a2_ref, 1)
    q0_ref[...] = jnp.zeros_like(q0_ref)
    q1_ref[...] = jnp.zeros_like(q1_ref)

    def weighted_shifts(half, z):
        pieces = [wall[(half * 4 + z) * 4 + y_].astype(F32) for y_ in range(4)]
        for v in range(6):
            row, col = 8 * (v % 3 // 2), 128 * (v % 3 % 2)
            lo, hi = [pieces[y_][row : row + 8, col : col + 128] for y_ in (v // 3, 2 + v // 3)]
            adjoint_shifts(t2_ref, half, v, lo, hi)

    def gather(step):
        z = (zh + jnp.where(step == 0, 0, jnp.where(step == 1, 1, jnp.where(step == 2, 3, 2)))) % 4
        for dy in (1, 3, 2, 0):
            at = (y + dy) % 4

            @pl.when((step > 0) | (dy > 0))
            def _():
                arrive(wall.at[(core * 4 + z) * 4 + at], w_recv.at[z * 4 + at])

        block = wall.at[pl.ds((core * 4 + z) * 4, 4)]
        send(block, block, wc_send.at[z], wc_recv.at[z], partner)
        weighted_shifts(core, z)
        other = wall.at[pl.ds(((1 - core) * 4 + z) * 4, 4)]
        arrive(other, wc_recv.at[z])
        weighted_shifts(1 - core, z)
        return z

    @pl.loop(0, 3)
    def _(step):
        z = gather(step)
        q0_ref[...] += jnp.dot(a2_ref[z], t2_ref[...], preferred_element_type=F32)
        q1_ref[...] += jnp.dot(a2_ref[z, :, :256], t2_ref[256:, :], preferred_element_type=F32)

    z = gather(3)
    for part in range(2):
        to_half = ms // 4 if part else 1 - ms // 4
        rows = pl.ds(pl.multiple_of(256 * to_half, 256), 256)
        q0_ref[rows, :] += jnp.dot(a2_ref[z, rows, :], t2_ref[...], preferred_element_type=F32)
        q1_ref[rows, :] += jnp.dot(a2_ref[z, rows, :256], t2_ref[256:, :], preferred_element_type=F32)

        @pl.loop(0, 4)
        def _(r):
            for v in range(6):
                lo, hi = folded(earlier, q0_ref, q1_ref, pl.multiple_of(256 * to_half + 8 * r, 8), 32, v)
                gf[part, r, :, 128 * v : 128 * v + 128] = jnp.concatenate([lo, hi], 0)

        for k in (2, 1, 3, 0):
            to = (ms + k) % 4
            if part and k == 0:
                continue
            slot = to_half * 4 + to
            gmsg[slot] = gf[part, to].astype(BF16)
            sent.append(
                send(gmsg.at[slot], grecv.at[ms], g_send.at[4 * part + k], g_recv.at[ms], sensor_at(slot))
            )

    total = gf[1, ms % 4]
    for k in (1, 3, 2):
        at = (ms // 4) * 4 + (ms + k) % 4
        arrive(grecv.at[at], g_recv.at[at])
        total = total + grecv[at].astype(F32)
    for k in range(4):
        at = (1 - ms // 4) * 4 + (ms + k) % 4
        arrive(grecv.at[at], g_recv.at[at])
        total = total + grecv[at].astype(F32)
    for v in range(6):
        for t in range(2):
            out_ref[8 * v : 8 * v + 8, 128 * t : 128 * t + 128] = total[8 * t : 8 * t + 8, 128 * v : 128 * v + 128]

    for copy in sent:
        copy.wait_send()

    @pl.loop(0, 4)
    def _(b):
        sent_off(ybuf.at[b, 0], c_send.at[b])
        sent_off(wall.at[pl.ds((core * 4 + b) * 4, 4)], wc_send.at[b])
        for dy in range(4):

            @pl.when((b < 3) | (dy > 0))
            def _():
                sent_off(ybuf.at[b, 1, (y + dy) % 4], z_send.at[b, dy])


def shards(histories, kernel, noise_weight):
    V, S = pltpu.VMEM, pltpu.SemaphoreType.DMA
    out = pl.pallas_call(
        body,
        out_shape=jax.ShapeDtypeStruct((48, 256), F32),
        in_specs=[pl.BlockSpec(memory_space=pltpu.HBM)] * 3,
        out_specs=pl.BlockSpec(memory_space=pltpu.VMEM),
        scratch_shapes=[
            V((64, 64, 256), BF16), V((64, 256), F32), V((2, 4608, 128), F32), V((2, 512, 1024), BF16),
            V((1024, 1024), BF16), V((4, 128, 2048), BF16), V((4, 512, 512), BF16), V((2048, 768), BF16),
            V((128, 768), F32), V((128, 768), F32), V((512, 768), BF16), V((512, 768), F32), V((512, 768), F32),
            V((8, 48, 256), BF16), V((4, 2, 4, 8, 384), F32), V((4, 4, 8, 384), F32), V((16, 8, 384), F32),
            V((32, 16, 256), BF16), V((2, 4, 16, 768), F32), V((8, 16, 768), BF16), V((8, 16, 768), BF16),
            S((6,)), S((8,)), S((8,)), S((4,)), S((4,)), S((4, 4)), S((16,)), S((16,)), S((16,)), S((4,)), S((4,)),
            S((8,)), S((8,)),
        ],
        compiler_params=pltpu.CompilerParams(
            collective_id=0, has_side_effects=True, vmem_limit_bytes=60 * 2**20
        ),
        cost_estimate=pl.CostEstimate(flops=4831838208, bytes_accessed=2300000, transcendentals=0),
        name="hessian",
    )(kernel, histories.transpose(1, 0, 2).reshape(48, 256), noise_weight)
    return out.reshape(6, 8, 256).transpose(1, 0, 2)


def solution(mesh):
    in_specs = (P(("param", "sensor"), None, None), P("sensor", "param", None), P("sensor", None))
    out_specs = P(("param", "sensor"), None, None)
    return jax.shard_map(shards, mesh=mesh, in_specs=in_specs, out_specs=out_specs, check_vma=False)
```

```python
import jax
import jax.numpy as jnp
from jax import lax
from jax.experimental import pallas as pl
from jax.experimental.pallas import tpu as pltpu
from jax.sharding import PartitionSpec as P

F32, BF16 = jnp.float32, jnp.bfloat16
MESH = pl.DeviceIdType.MESH


def lane_of(rows):
    return lax.broadcasted_iota(jnp.int32, (rows, 128), 1)


def fill_order(order_ref):
    row, col = [lax.broadcasted_iota(jnp.int32, (128, 1024), d) for d in (0, 1)]
    low = row & 7
    target = low * 128 + (row - low)

    @pl.loop(0, 8)
    def _(j):
        here = jnp.where(col == target + j, 1.0, 0.0).astype(BF16)
        order_ref[pl.ds(pl.multiple_of(j * 128, 128), 128), :] = here


def reordered(x, order_ref, n):
    return jnp.dot(x, order_ref[:, pl.ds(pl.multiple_of(n * 256, 256), 256)], preferred_element_type=F32)


def forward_taps(k_ref, wide_ref, x_ref, order_ref, a_ref):
    for h in range(2):

        @pl.loop(0, 8)
        def _(g):
            row = pl.ds(pl.multiple_of(64 * g, 64), 64)
            for j in range(8):
                x_ref[h, row, 128 * j : 128 * j + 128] = wide_ref[h, pl.ds(8 * g + j, 64, stride=72), :].astype(BF16)

    @pl.loop(0, 8)
    def _(step):
        h, n = step // 4, step % 4
        ys = reordered(x_ref[h], order_ref, n)
        for z in range(4):
            for g in range(8):
                for c in range(2):
                    first = 64 * g + 8 * z
                    part = [ys[r : r + 8, 128 * c : 128 * c + 128] for r in (first, first + 32)]
                    row = pl.ds(pl.multiple_of((2 * n + c) * 16, 16), 16)
                    col = pl.ds(pl.multiple_of(h * 1024 + g * 128, 128), 128)
                    a_ref[z, row, col] = jnp.concatenate(part, 0).astype(BF16)


def adjoint_taps(k_ref, order_ref, a_ref, h):
    @pl.loop(0, 4)
    def _(n):
        x = [
            jnp.concatenate([k_ref[8 * g + i, :, 128 * h : 128 * h + 128] for g in range(8)], 0) for i in range(8)
        ]
        ys = reordered(jnp.concatenate(x, 1), order_ref, n)
        for to in range(2):
            for g in range(8):
                for c in range(2):
                    first = 64 * g + 32 * to
                    row = pl.ds(pl.multiple_of(256 * to + (2 * n + c) * 32, 32), 32)
                    a_ref[g % 4, row, 256 * h + 128 * (g // 4) : 256 * h + 128 * (g // 4) + 128] = ys[
                        first : first + 32, 128 * c : 128 * c + 128
                    ].astype(BF16)


def put_shifts(t_ref, rows, v, series):
    col = pl.ds(v * 128, 128)
    for start, shifted in zip(rows, series):
        for q in range(8):
            row = pl.multiple_of(start + 16 * q, 16)
            t_ref[pl.ds(row, 16), col] = jnp.concatenate(shifted[2 * q : 2 * q + 2], 0).astype(BF16)


def later(lo, hi, s):
    if s == 0:
        return lo, hi
    lane = lane_of(lo.shape[0])
    a, b = pltpu.roll(lo, s, 1), pltpu.roll(hi, s, 1)
    return jnp.where(lane < s, 0.0, a), jnp.where(lane < s, a, b)


def earlier(lo, hi, s):
    if s == 0:
        return lo, hi
    lane = lane_of(lo.shape[0])
    a, b = pltpu.roll(lo, 128 - s, 1), pltpu.roll(hi, 128 - s, 1)
    return jnp.where(lane < 128 - s, a, b), jnp.where(lane < 128 - s, b, 0.0)


def forward_shifts(t_ref, g, v, lo, hi):
    pairs = [later(lo, hi, 8 * l) for l in range(16)]
    put_shifts(t_ref, (1024 + g * 128, g * 128), v, zip(*pairs))


def adjoint_shifts(t_ref, half, v, lo, hi):
    pairs = [earlier(lo, hi, 8 * l) for l in range(16)]
    put_shifts(t_ref, (half * 128, 256 + half * 128), v, zip(*pairs))


def folded(shift, lo_ref, hi_ref, start, stride, v):
    col = slice(128 * v, 128 * v + 128)
    lo = hi = None
    for c in range(8):
        row = pl.ds(start + stride * c, 8)
        a, b = shift(lo_ref[row, col], hi_ref[row, col], c)
        lo, hi = (a, b) if lo is None else (lo + a, hi + b)
    return lo, hi


def body(
    k_hbm, hist_hbm, noise_hbm, out_ref,
    k_ref, noise_ref, wide_ref, x_ref, order_ref, a1_ref, a2_ref, t1_ref, long_ref, short_ref, t2_ref, q0_ref, q1_ref,
    hb, ybuf, yrecv, zrecv, wall, gf, gmsg, grecv,
    load_sem, told, h_send, h_recv, c_send, c_recv, z_send, z_recv, w_send, w_recv, wc_send, wc_recv, g_send, g_recv,
):
    ms, mp = lax.axis_index("sensor"), lax.axis_index("param")
    zh, y, core = mp // 8, (mp // 2) % 4, mp % 2

    def sensor_at(s):
        return {"sensor": s, "param": mp}

    def param_at(z_, y_, core_):
        return {"sensor": ms, "param": z_ * 8 + y_ * 2 + core_}

    partner = param_at(zh, y, 1 - core)

    pltpu.make_async_copy(hist_hbm, hb.at[ms], load_sem.at[0]).start()
    k_loads = []
    for part in range(4):
        rows = pl.ds(16 * part, 16)
        k_loads.append(pltpu.make_async_copy(k_hbm.at[rows], k_ref.at[rows], load_sem.at[2 + part]))
        k_loads[-1].start()
    pltpu.make_async_copy(noise_hbm, noise_ref, load_sem.at[1]).start()

    barrier = pltpu.get_barrier_semaphore()
    peers = [sensor_at((ms + k) % 8) for k in range(1, 8)]
    peers += [partner]
    peers += [param_at(zh, (y + dy) % 4, core) for dy in range(1, 4)]
    beside = [param_at((zh + dz) % 4, y, core) for dz in (1, 3)]
    peers += beside
    for peer in peers:
        pl.semaphore_signal(barrier, inc=1, device_id=peer, device_id_type=MESH)

    fill_order(order_ref)
    pltpu.make_async_copy(hist_hbm, hb.at[ms], load_sem.at[0]).wait()
    pl.semaphore_wait(barrier, len(peers))
    for peer in beside:
        pl.semaphore_signal(told.at[0], inc=1, device_id=peer, device_id_type=MESH)

    def send(src, dst, send_sem, recv_sem, peer):
        copy = pltpu.make_async_remote_copy(
            src_ref=src, dst_ref=dst, send_sem=send_sem, recv_sem=recv_sem, device_id=peer, device_id_type=MESH
        )
        copy.start()
        return copy

    def arrive(dst, recv_sem):
        pltpu.make_async_remote_copy(
            src_ref=dst, dst_ref=dst, send_sem=recv_sem, recv_sem=recv_sem, device_id=partner, device_id_type=MESH
        ).wait_recv()

    def sent_off(src, send_sem):
        pltpu.make_async_remote_copy(
            src_ref=src, dst_ref=src, send_sem=send_sem, recv_sem=send_sem, device_id=partner, device_id_type=MESH
        ).wait_send()

    sent = []
    for k in (2, 6, 1, 3, 5, 7, 4):
        sent.append(send(hb.at[ms], hb.at[ms], h_send.at[k], h_recv.at[ms], sensor_at((ms + k) % 8)))

    for part in range(4):
        k_loads[part].wait()

        @pl.loop(8 * part, 8 * part + 8)
        def _(step):
            for u in range(2):
                i = 2 * step + u
                for h in range(2):
                    wide_ref[h, pl.ds(pl.multiple_of(i * 72, 8), 64), :] = k_ref[i, :, 128 * h : 128 * h + 128].astype(F32)

    forward_taps(k_ref, wide_ref, x_ref, order_ref, a1_ref)

    pl.semaphore_wait(told.at[0], 2)
    for peer in beside:
        pl.semaphore_signal(told.at[1], inc=1, device_id=peer, device_id_type=MESH)

    @pl.loop(0, 8)
    def _(k):
        s = (ms + k) % 8

        @pl.when(k > 0)
        def _():
            arrive(hb.at[s], h_recv.at[s])

        block = hb[s].astype(F32)
        for v in range(6):
            forward_shifts(t1_ref, s, v, block[8 * v : 8 * v + 8, :128], block[8 * v : 8 * v + 8, 128:])

    def z_of(b):
        return (zh + jnp.where(b == 0, 2, jnp.where(b == 1, 1, jnp.where(b == 2, 3, 0)))) % 4

    def pass_on(b, dys):
        arrive(yrecv.at[b], c_recv.at[b])
        for dy in dys:
            to = (y + dy) % 4
            ybuf[b, 1, to] = ybuf[b, 1, to] + yrecv[b, to]
            send(
                ybuf.at[b, 1, to], zrecv.at[zh * 4 + y], z_send.at[b, dy], z_recv.at[zh * 4 + y],
                param_at(z_of(b), to, core),
            )

    @pl.loop(0, 4)
    def _(b):
        z = z_of(b)
        long_ref[...] = jnp.dot(a1_ref[z], t1_ref[...], preferred_element_type=F32)
        short_ref[...] = jnp.dot(a1_ref[z, :, :1024], t1_ref[1024:, :], preferred_element_type=F32)
        for half in range(2):
            mine = (half + core + 1) % 2
            for v in range(6):
                lo, hi = folded(later, short_ref, long_ref, 8 * half, 16, v)
                col = slice(128 * (v % 3), 128 * (v % 3) + 128)
                ybuf[b, mine, v // 3, :, col] = lo
                ybuf[b, mine, 2 + v // 3, :, col] = hi
        send(ybuf.at[b, 0], yrecv.at[b], c_send.at[b], c_recv.at[b], partner)

        @pl.when(b == 1)
        def _():
            pl.semaphore_wait(told.at[1], 2)

        @pl.when(b > 0)
        def _():
            pass_on(b - 1, (2, 1, 3, 0))

    pass_on(3, (2, 1, 3))

    adjoint_taps(k_ref, order_ref, a2_ref, 0)

    piece = ybuf[3, 1, y] + yrecv[3, y]
    for dz in (2, 1, 3, 0):
        for dy in range(4):
            if dz or dy:
                at = ((zh + dz) % 4) * 4 + (y + dy) % 4
                arrive(zrecv.at[at], z_recv.at[at])
                piece = piece + zrecv[at]

    pltpu.make_async_copy(noise_hbm, noise_ref, load_sem.at[1]).wait()
    group = core * 4 + zh
    noise = noise_ref[pl.ds(pl.multiple_of(8 * group, 8), 8), pl.ds(pl.multiple_of(128 * (y // 2), 128), 128)]
    tiles = [piece[:, 128 * k : 128 * k + 128] * noise for k in range(3)]
    tiles.append(jnp.zeros_like(noise))
    here = group * 4 + y
    wall[here] = jnp.concatenate(
        [jnp.concatenate(tiles[:2], 1), jnp.concatenate(tiles[2:], 1)], 0
    ).astype(BF16)
    for dz in (2, 1, 3, 0):
        for dy in (2, 1, 3, 0):
            if dz or dy:
                peer = param_at((zh + dz) % 4, (y + dy) % 4, core)
                sent.append(send(wall.at[here], wall.at[here], w_send.at[dz * 4 + dy], w_recv.at[zh * 4 + y], peer))

    adjoint_taps(k_ref, order_ref, a2_ref, 1)
    q0_ref[...] = jnp.zeros_like(q0_ref)
    q1_ref[...] = jnp.zeros_like(q1_ref)

    def weighted_shifts(half, z):
        pieces = [wall[(half * 4 + z) * 4 + y_].astype(F32) for y_ in range(4)]
        for v in range(6):
            row, col = 8 * (v % 3 // 2), 128 * (v % 3 % 2)
            lo, hi = [pieces[y_][row : row + 8, col : col + 128] for y_ in (v // 3, 2 + v // 3)]
            adjoint_shifts(t2_ref, half, v, lo, hi)

    def gather(step):
        z = (zh + jnp.where(step == 0, 0, jnp.where(step == 1, 1, jnp.where(step == 2, 3, 2)))) % 4
        for dy in (1, 3, 2, 0):
            at = (y + dy) % 4

            @pl.when((step > 0) | (dy > 0))
            def _():
                arrive(wall.at[(core * 4 + z) * 4 + at], w_recv.at[z * 4 + at])

        block = wall.at[pl.ds((core * 4 + z) * 4, 4)]
        send(block, block, wc_send.at[z], wc_recv.at[z], partner)
        weighted_shifts(core, z)
        other = wall.at[pl.ds(((1 - core) * 4 + z) * 4, 4)]
        arrive(other, wc_recv.at[z])
        weighted_shifts(1 - core, z)
        return z

    @pl.loop(0, 3)
    def _(step):
        z = gather(step)
        q0_ref[...] += jnp.dot(a2_ref[z], t2_ref[...], preferred_element_type=F32)
        q1_ref[...] += jnp.dot(a2_ref[z, :, :256], t2_ref[256:, :], preferred_element_type=F32)

    z = gather(3)
    for part in range(2):
        to_half = ms // 4 if part else 1 - ms // 4
        rows = pl.ds(pl.multiple_of(256 * to_half, 256), 256)
        q0_ref[rows, :] += jnp.dot(a2_ref[z, rows, :], t2_ref[...], preferred_element_type=F32)
        q1_ref[rows, :] += jnp.dot(a2_ref[z, rows, :256], t2_ref[256:, :], preferred_element_type=F32)

        @pl.loop(0, 4)
        def _(r):
            for v in range(6):
                lo, hi = folded(earlier, q0_ref, q1_ref, pl.multiple_of(256 * to_half + 8 * r, 8), 32, v)
                gf[part, r, :, 128 * v : 128 * v + 128] = jnp.concatenate([lo, hi], 0)

        for k in (2, 1, 3, 0):
            to = (ms + k) % 4
            if part and k == 0:
                continue
            slot = to_half * 4 + to
            gmsg[slot] = gf[part, to].astype(BF16)
            sent.append(
                send(gmsg.at[slot], grecv.at[ms], g_send.at[4 * part + k], g_recv.at[ms], sensor_at(slot))
            )

    total = gf[1, ms % 4]
    for k in (1, 3, 2):
        at = (ms // 4) * 4 + (ms + k) % 4
        arrive(grecv.at[at], g_recv.at[at])
        total = total + grecv[at].astype(F32)
    for k in range(4):
        at = (1 - ms // 4) * 4 + (ms + k) % 4
        arrive(grecv.at[at], g_recv.at[at])
        total = total + grecv[at].astype(F32)
    for v in range(6):
        for t in range(2):
            out_ref[8 * v : 8 * v + 8, 128 * t : 128 * t + 128] = total[8 * t : 8 * t + 8, 128 * v : 128 * v + 128]

    for copy in sent:
        copy.wait_send()

    @pl.loop(0, 4)
    def _(b):
        sent_off(ybuf.at[b, 0], c_send.at[b])
        sent_off(wall.at[pl.ds((core * 4 + b) * 4, 4)], wc_send.at[b])
        for dy in range(4):

            @pl.when((b < 3) | (dy > 0))
            def _():
                sent_off(ybuf.at[b, 1, (y + dy) % 4], z_send.at[b, dy])


def shards(histories, kernel, noise_weight):
    V, S = pltpu.VMEM, pltpu.SemaphoreType.DMA
    out = pl.pallas_call(
        body,
        out_shape=jax.ShapeDtypeStruct((48, 256), F32),
        in_specs=[pl.BlockSpec(memory_space=pltpu.HBM)] * 3,
        out_specs=pl.BlockSpec(memory_space=pltpu.VMEM),
        scratch_shapes=[
            V((64, 64, 256), BF16), V((64, 256), F32), V((2, 4608, 128), F32), V((2, 512, 1024), BF16),
            V((1024, 1024), BF16), V((4, 128, 2048), BF16), V((4, 512, 512), BF16), V((2048, 768), BF16),
            V((128, 768), F32), V((128, 768), F32), V((512, 768), BF16), V((512, 768), F32), V((512, 768), F32),
            V((8, 48, 256), BF16), V((4, 2, 4, 8, 384), F32), V((4, 4, 8, 384), F32), V((16, 8, 384), F32),
            V((32, 16, 256), BF16), V((2, 4, 16, 768), F32), V((8, 16, 768), BF16), V((8, 16, 768), BF16),
            S((6,)), pltpu.SemaphoreType.REGULAR((2,)), S((8,)), S((8,)), S((4,)), S((4,)), S((4, 4)), S((16,)), S((16,)), S((16,)), S((4,)), S((4,)),
            S((8,)), S((8,)),
        ],
        compiler_params=pltpu.CompilerParams(
            collective_id=0, has_side_effects=True, vmem_limit_bytes=60 * 2**20
        ),
        cost_estimate=pl.CostEstimate(flops=4831838208, bytes_accessed=2300000, transcendentals=0),
        name="hessian",
    )(kernel, histories.transpose(1, 0, 2).reshape(48, 256), noise_weight)
    return out.reshape(6, 8, 256).transpose(1, 0, 2)


def solution(mesh):
    in_specs = (P(("param", "sensor"), None, None), P("sensor", "param", None), P("sensor", None))
    out_specs = P(("param", "sensor"), None, None)
    return jax.shard_map(shards, mesh=mesh, in_specs=in_specs, out_specs=out_specs, check_vma=False)
```

```python
import jax
import jax.numpy as jnp
from jax import lax
from jax.experimental import pallas as pl
from jax.experimental.pallas import tpu as pltpu
from jax.sharding import PartitionSpec as P

F32, BF16 = jnp.float32, jnp.bfloat16
MESH = pl.DeviceIdType.MESH


def lane_of(rows):
    return lax.broadcasted_iota(jnp.int32, (rows, 128), 1)


def fill_order(order_ref):
    row, col = [lax.broadcasted_iota(jnp.int32, (128, 1024), d) for d in (0, 1)]
    low = row & 7
    target = low * 128 + (row - low)

    @pl.loop(0, 8)
    def _(j):
        here = jnp.where(col == target + j, 1.0, 0.0).astype(BF16)
        order_ref[pl.ds(pl.multiple_of(j * 128, 128), 128), :] = here


def reordered(x, order_ref, n):
    return jnp.dot(x, order_ref[:, pl.ds(pl.multiple_of(n * 256, 256), 256)], preferred_element_type=F32)


def forward_taps(k_ref, wide_ref, x_ref, order_ref, a_ref):
    for h in range(2):

        @pl.loop(0, 8)
        def _(g):
            row = pl.ds(pl.multiple_of(64 * g, 64), 64)
            for j in range(8):
                x_ref[h, row, 128 * j : 128 * j + 128] = wide_ref[h, pl.ds(8 * g + j, 64, stride=72), :].astype(BF16)

    @pl.loop(0, 8)
    def _(step):
        h, n = step // 4, step % 4
        ys = reordered(x_ref[h], order_ref, n)
        for z in range(4):
            for g in range(8):
                for c in range(2):
                    first = 64 * g + 8 * z
                    part = [ys[r : r + 8, 128 * c : 128 * c + 128] for r in (first, first + 32)]
                    row = pl.ds(pl.multiple_of((2 * n + c) * 16, 16), 16)
                    col = pl.ds(pl.multiple_of(h * 1024 + g * 128, 128), 128)
                    a_ref[z, row, col] = jnp.concatenate(part, 0).astype(BF16)


def adjoint_taps(k_ref, order_ref, a_ref, h):
    @pl.loop(0, 4)
    def _(n):
        x = [
            jnp.concatenate([k_ref[8 * g + i, :, 128 * h : 128 * h + 128] for g in range(8)], 0) for i in range(8)
        ]
        ys = reordered(jnp.concatenate(x, 1), order_ref, n)
        for to in range(2):
            for g in range(8):
                for c in range(2):
                    first = 64 * g + 32 * to
                    row = pl.ds(pl.multiple_of(256 * to + (2 * n + c) * 32, 32), 32)
                    a_ref[g % 4, row, 256 * h + 128 * (g // 4) : 256 * h + 128 * (g // 4) + 128] = ys[
                        first : first + 32, 128 * c : 128 * c + 128
                    ].astype(BF16)


def put_shifts(t_ref, rows, v, series):
    col = pl.ds(v * 128, 128)
    for start, shifted in zip(rows, series):
        for q in range(8):
            row = pl.multiple_of(start + 16 * q, 16)
            t_ref[pl.ds(row, 16), col] = jnp.concatenate(shifted[2 * q : 2 * q + 2], 0).astype(BF16)


def later(lo, hi, s):
    if s == 0:
        return lo, hi
    lane = lane_of(lo.shape[0])
    a, b = pltpu.roll(lo, s, 1), pltpu.roll(hi, s, 1)
    return jnp.where(lane < s, 0.0, a), jnp.where(lane < s, a, b)


def earlier(lo, hi, s):
    if s == 0:
        return lo, hi
    lane = lane_of(lo.shape[0])
    a, b = pltpu.roll(lo, 128 - s, 1), pltpu.roll(hi, 128 - s, 1)
    return jnp.where(lane < 128 - s, a, b), jnp.where(lane < 128 - s, b, 0.0)


def forward_shifts(t_ref, g, v, lo, hi):
    pairs = [later(lo, hi, 8 * l) for l in range(16)]
    put_shifts(t_ref, (1024 + g * 128, g * 128), v, zip(*pairs))


def adjoint_shifts(t_ref, half, v, lo, hi):
    pairs = [earlier(lo, hi, 8 * l) for l in range(16)]
    put_shifts(t_ref, (half * 128, 256 + half * 128), v, zip(*pairs))


def folded(shift, lo_ref, hi_ref, start, stride, v):
    col = slice(128 * v, 128 * v + 128)
    lo = hi = None
    for c in range(8):
        row = pl.ds(start + stride * c, 8)
        a, b = shift(lo_ref[row, col], hi_ref[row, col], c)
        lo, hi = (a, b) if lo is None else (lo + a, hi + b)
    return lo, hi


def body(
    k_hbm, hist_hbm, noise_hbm, out_ref,
    k_ref, noise_ref, wide_ref, x_ref, order_ref, a1_ref, a2_ref, t1_ref, long_ref, short_ref, t2_ref, q0_ref, q1_ref,
    hb, ybuf, yrecv, zrecv, wall, gf, gmsg, grecv,
    load_sem, told, h_send, h_recv, c_send, c_recv, z_send, z_recv, w_send, w_recv, wc_send, wc_recv, g_send, g_recv,
):
    ms, mp = lax.axis_index("sensor"), lax.axis_index("param")
    zh, y, core = mp // 8, (mp // 2) % 4, mp % 2

    def sensor_at(s):
        return {"sensor": s, "param": mp}

    def param_at(z_, y_, core_):
        return {"sensor": ms, "param": z_ * 8 + y_ * 2 + core_}

    partner = param_at(zh, y, 1 - core)

    pltpu.make_async_copy(hist_hbm, hb.at[ms], load_sem.at[0]).start()
    k_loads = []
    for part in range(4):
        rows = pl.ds(16 * part, 16)
        k_loads.append(pltpu.make_async_copy(k_hbm.at[rows], k_ref.at[rows], load_sem.at[2 + part]))
        k_loads[-1].start()
    pltpu.make_async_copy(noise_hbm, noise_ref, load_sem.at[1]).start()

    barrier = pltpu.get_barrier_semaphore()
    peers = [sensor_at((ms + k) % 8) for k in range(1, 8)]
    peers += [partner]
    peers += [param_at(zh, (y + dy) % 4, core) for dy in range(1, 4)]
    beside = [param_at((zh + dz) % 4, y, core) for dz in (1, 3)]
    peers += beside
    for peer in peers:
        pl.semaphore_signal(barrier, inc=1, device_id=peer, device_id_type=MESH)

    fill_order(order_ref)
    pltpu.make_async_copy(hist_hbm, hb.at[ms], load_sem.at[0]).wait()
    pl.semaphore_wait(barrier, len(peers))
    for peer in beside:
        pl.semaphore_signal(told.at[0], inc=1, device_id=peer, device_id_type=MESH)

    def send(src, dst, send_sem, recv_sem, peer):
        copy = pltpu.make_async_remote_copy(
            src_ref=src, dst_ref=dst, send_sem=send_sem, recv_sem=recv_sem, device_id=peer, device_id_type=MESH
        )
        copy.start()
        return copy

    def arrive(dst, recv_sem):
        pltpu.make_async_remote_copy(
            src_ref=dst, dst_ref=dst, send_sem=recv_sem, recv_sem=recv_sem, device_id=partner, device_id_type=MESH
        ).wait_recv()

    def sent_off(src, send_sem):
        pltpu.make_async_remote_copy(
            src_ref=src, dst_ref=src, send_sem=send_sem, recv_sem=send_sem, device_id=partner, device_id_type=MESH
        ).wait_send()

    sent = []
    for dz, dx in ((1, 2), (1, 1), (1, 3), (0, 2), (1, 0), (0, 1), (0, 3)):
        peer = sensor_at((ms // 4 + dz) % 2 * 4 + (ms + dx) % 4)
        sent.append(send(hb.at[ms], hb.at[ms], h_send.at[4 * dz + dx], h_recv.at[ms], peer))

    for part in range(4):
        k_loads[part].wait()

        @pl.loop(8 * part, 8 * part + 8)
        def _(step):
            for u in range(2):
                i = 2 * step + u
                for h in range(2):
                    wide_ref[h, pl.ds(pl.multiple_of(i * 72, 8), 64), :] = k_ref[i, :, 128 * h : 128 * h + 128].astype(F32)

    forward_taps(k_ref, wide_ref, x_ref, order_ref, a1_ref)

    pl.semaphore_wait(told.at[0], 2)
    for peer in beside:
        pl.semaphore_signal(told.at[1], inc=1, device_id=peer, device_id_type=MESH)

    @pl.loop(0, 8)
    def _(k):
        dz = jnp.where(k == 3, 1, k // 5)
        dx = jnp.where(k == 4, 2, jnp.where(k == 7, 2, jnp.where((k == 1) | (k == 5), 1, jnp.where((k == 2) | (k == 6), 3, 0))))
        s = (ms // 4 + dz) % 2 * 4 + (ms + dx) % 4

        @pl.when(k > 0)
        def _():
            arrive(hb.at[s], h_recv.at[s])

        block = hb[s].astype(F32)
        for v in range(6):
            forward_shifts(t1_ref, s, v, block[8 * v : 8 * v + 8, :128], block[8 * v : 8 * v + 8, 128:])

    def z_of(b):
        return (zh + jnp.where(b == 0, 2, jnp.where(b == 1, 1, jnp.where(b == 2, 3, 0)))) % 4

    def pass_on(b, dys):
        arrive(yrecv.at[b], c_recv.at[b])
        for dy in dys:
            to = (y + dy) % 4
            ybuf[b, 1, to] = ybuf[b, 1, to] + yrecv[b, to]
            send(
                ybuf.at[b, 1, to], zrecv.at[zh * 4 + y], z_send.at[b, dy], z_recv.at[zh * 4 + y],
                param_at(z_of(b), to, core),
            )

    @pl.loop(0, 4)
    def _(b):
        z = z_of(b)
        long_ref[...] = jnp.dot(a1_ref[z], t1_ref[...], preferred_element_type=F32)
        short_ref[...] = jnp.dot(a1_ref[z, :, :1024], t1_ref[1024:, :], preferred_element_type=F32)
        for half in range(2):
            mine = (half + core + 1) % 2
            for v in range(6):
                lo, hi = folded(later, short_ref, long_ref, 8 * half, 16, v)
                col = slice(128 * (v % 3), 128 * (v % 3) + 128)
                ybuf[b, mine, v // 3, :, col] = lo
                ybuf[b, mine, 2 + v // 3, :, col] = hi
        send(ybuf.at[b, 0], yrecv.at[b], c_send.at[b], c_recv.at[b], partner)

        @pl.when(b == 1)
        def _():
            pl.semaphore_wait(told.at[1], 2)

        @pl.when(b > 0)
        def _():
            pass_on(b - 1, (2, 1, 3, 0))

    pass_on(3, (2, 1, 3))

    adjoint_taps(k_ref, order_ref, a2_ref, 0)

    piece = ybuf[3, 1, y] + yrecv[3, y]
    for dz in (2, 1, 3, 0):
        for dy in range(4):
            if dz or dy:
                at = ((zh + dz) % 4) * 4 + (y + dy) % 4
                arrive(zrecv.at[at], z_recv.at[at])
                piece = piece + zrecv[at]

    pltpu.make_async_copy(noise_hbm, noise_ref, load_sem.at[1]).wait()
    group = core * 4 + zh
    noise = noise_ref[pl.ds(pl.multiple_of(8 * group, 8), 8), pl.ds(pl.multiple_of(128 * (y // 2), 128), 128)]
    tiles = [piece[:, 128 * k : 128 * k + 128] * noise for k in range(3)]
    tiles.append(jnp.zeros_like(noise))
    here = group * 4 + y
    wall[here] = jnp.concatenate(
        [jnp.concatenate(tiles[:2], 1), jnp.concatenate(tiles[2:], 1)], 0
    ).astype(BF16)
    for dz in (2, 1, 3, 0):
        for dy in (2, 1, 3, 0):
            if dz or dy:
                peer = param_at((zh + dz) % 4, (y + dy) % 4, core)
                sent.append(send(wall.at[here], wall.at[here], w_send.at[dz * 4 + dy], w_recv.at[zh * 4 + y], peer))

    adjoint_taps(k_ref, order_ref, a2_ref, 1)
    q0_ref[...] = jnp.zeros_like(q0_ref)
    q1_ref[...] = jnp.zeros_like(q1_ref)

    def weighted_shifts(half, z):
        pieces = [wall[(half * 4 + z) * 4 + y_].astype(F32) for y_ in range(4)]
        for v in range(6):
            row, col = 8 * (v % 3 // 2), 128 * (v % 3 % 2)
            lo, hi = [pieces[y_][row : row + 8, col : col + 128] for y_ in (v // 3, 2 + v // 3)]
            adjoint_shifts(t2_ref, half, v, lo, hi)

    def z_in(step):
        return (zh + jnp.where(step == 0, 0, jnp.where(step == 1, 1, jnp.where(step == 2, 3, 2)))) % 4

    def fetch(step):
        z = z_in(step)
        for dy in (1, 3, 2, 0):
            at = (y + dy) % 4

            @pl.when((step > 0) | (dy > 0))
            def _():
                arrive(wall.at[(core * 4 + z) * 4 + at], w_recv.at[z * 4 + at])

        block = wall.at[pl.ds((core * 4 + z) * 4, 4)]
        send(block, block, wc_send.at[z], wc_recv.at[z], partner)

    def other_half(z):
        arrive(wall.at[pl.ds(((1 - core) * 4 + z) * 4, 4)], wc_recv.at[z])
        weighted_shifts(1 - core, z)

    fetch(0)

    @pl.loop(0, 4)
    def _(step):
        z = z_in(step)
        weighted_shifts(core, z)

        @pl.when(step < 3)
        def _():
            fetch(step + 1)

        other_half(z)

        @pl.when(step < 3)
        def _():
            q0_ref[...] += jnp.dot(a2_ref[z], t2_ref[...], preferred_element_type=F32)
            q1_ref[...] += jnp.dot(a2_ref[z, :, :256], t2_ref[256:, :], preferred_element_type=F32)

    @pl.loop(0, 2)
    def _(part):
        z = z_in(3)
        to_half = (ms // 4 + 1 + part) % 2
        rows = pl.ds(pl.multiple_of(256 * to_half, 256), 256)
        q0_ref[rows, :] += jnp.dot(a2_ref[z, rows, :], t2_ref[...], preferred_element_type=F32)
        q1_ref[rows, :] += jnp.dot(a2_ref[z, rows, :256], t2_ref[256:, :], preferred_element_type=F32)

        @pl.loop(0, 4)
        def _(r):
            for v in range(6):
                lo, hi = folded(earlier, q0_ref, q1_ref, pl.multiple_of(256 * to_half + 8 * r, 8), 32, v)
                gf[part, r, :, 128 * v : 128 * v + 128] = jnp.concatenate([lo, hi], 0)

        for k in (2, 1, 3, 0):
            slot = to_half * 4 + (ms + k) % 4

            @pl.when((part == 0) | (k > 0))
            def _():
                gmsg[slot] = gf[part, (ms + k) % 4].astype(BF16)
                send(gmsg.at[slot], grecv.at[ms], g_send.at[slot], g_recv.at[ms], sensor_at(slot))

    total = gf[1, ms % 4]
    for k in (1, 3, 2):
        at = (ms // 4) * 4 + (ms + k) % 4
        arrive(grecv.at[at], g_recv.at[at])
        total = total + grecv[at].astype(F32)
    for k in range(4):
        at = (1 - ms // 4) * 4 + (ms + k) % 4
        arrive(grecv.at[at], g_recv.at[at])
        total = total + grecv[at].astype(F32)
    for v in range(6):
        for t in range(2):
            out_ref[8 * v : 8 * v + 8, 128 * t : 128 * t + 128] = total[8 * t : 8 * t + 8, 128 * v : 128 * v + 128]

    for copy in sent:
        copy.wait_send()
    for k in range(1, 8):
        slot = (ms + k) % 8
        sent_off(gmsg.at[slot], g_send.at[slot])

    @pl.loop(0, 4)
    def _(b):
        sent_off(ybuf.at[b, 0], c_send.at[b])
        sent_off(wall.at[pl.ds((core * 4 + b) * 4, 4)], wc_send.at[b])
        for dy in range(4):

            @pl.when((b < 3) | (dy > 0))
            def _():
                sent_off(ybuf.at[b, 1, (y + dy) % 4], z_send.at[b, dy])


def shards(histories, kernel, noise_weight):
    V, S = pltpu.VMEM, pltpu.SemaphoreType.DMA
    out = pl.pallas_call(
        body,
        out_shape=jax.ShapeDtypeStruct((48, 256), F32),
        in_specs=[pl.BlockSpec(memory_space=pltpu.HBM)] * 3,
        out_specs=pl.BlockSpec(memory_space=pltpu.VMEM),
        scratch_shapes=[
            V((64, 64, 256), BF16), V((64, 256), F32), V((2, 4608, 128), F32), V((2, 512, 1024), BF16),
            V((1024, 1024), BF16), V((4, 128, 2048), BF16), V((4, 512, 512), BF16), V((2048, 768), BF16),
            V((128, 768), F32), V((128, 768), F32), V((512, 768), BF16), V((512, 768), F32), V((512, 768), F32),
            V((8, 48, 256), BF16), V((4, 2, 4, 8, 384), F32), V((4, 4, 8, 384), F32), V((16, 8, 384), F32),
            V((32, 16, 256), BF16), V((2, 4, 16, 768), F32), V((8, 16, 768), BF16), V((8, 16, 768), BF16),
            S((6,)), pltpu.SemaphoreType.REGULAR((2,)), S((8,)), S((8,)), S((4,)), S((4,)), S((4, 4)), S((16,)), S((16,)), S((16,)), S((4,)), S((4,)),
            S((8,)), S((8,)),
        ],
        compiler_params=pltpu.CompilerParams(
            collective_id=0, has_side_effects=True, vmem_limit_bytes=60 * 2**20
        ),
        cost_estimate=pl.CostEstimate(flops=4831838208, bytes_accessed=2300000, transcendentals=0),
        name="hessian",
    )(kernel, histories.transpose(1, 0, 2).reshape(48, 256), noise_weight)
    return out.reshape(6, 8, 256).transpose(1, 0, 2)


def solution(mesh):
    in_specs = (P(("param", "sensor"), None, None), P("sensor", "param", None), P("sensor", None))
    out_specs = P(("param", "sensor"), None, None)
    return jax.shard_map(shards, mesh=mesh, in_specs=in_specs, out_specs=out_specs, check_vma=False)
```

```python
import jax
import jax.numpy as jnp
from jax import lax
from jax.experimental import pallas as pl
from jax.experimental.pallas import tpu as pltpu
from jax.sharding import PartitionSpec as P

F32, BF16 = jnp.float32, jnp.bfloat16
MESH = pl.DeviceIdType.MESH


def lane_of(rows):
    return lax.broadcasted_iota(jnp.int32, (rows, 128), 1)


def fill_order(order_ref):
    row, col = [lax.broadcasted_iota(jnp.int32, (128, 1024), d) for d in (0, 1)]
    low = row & 7
    target = low * 128 + (row - low)

    @pl.loop(0, 8)
    def _(j):
        here = jnp.where(col == target + j, 1.0, 0.0).astype(BF16)
        order_ref[pl.ds(pl.multiple_of(j * 128, 128), 128), :] = here


def reordered(x, order_ref, n):
    return jnp.dot(x, order_ref[:, pl.ds(pl.multiple_of(n * 256, 256), 256)], preferred_element_type=F32)


def forward_taps(wide_ref, x_ref, order_ref, a_ref, beside, tell):
    for h in range(2):

        @pl.loop(0, 8)
        def _(g):
            row = pl.ds(pl.multiple_of(64 * g, 64), 64)
            for j in range(8):
                x_ref[h, row, 128 * j : 128 * j + 128] = wide_ref[h, pl.ds(8 * g + j, 64, stride=72), :].astype(BF16)

    def one(step):
        h, n = step // 4, step % 4
        ys = reordered(x_ref[h], order_ref, n)
        for z in range(4):
            for g in range(8):
                for c in range(2):
                    first = 64 * g + 8 * z
                    part = [ys[r : r + 8, 128 * c : 128 * c + 128] for r in (first, first + 32)]
                    row = pl.ds(pl.multiple_of((2 * n + c) * 16, 16), 16)
                    col = pl.ds(pl.multiple_of(h * 1024 + g * 128, 128), 128)
                    a_ref[z, row, col] = jnp.concatenate(part, 0).astype(BF16)

    pl.loop(0, 5)(one)
    tell()

    @pl.loop(5, 8)
    def _(step):
        beside(step)
        one(step)


def adjoint_taps(k_ref, order_ref, a_ref, h):
    @pl.loop(0, 4)
    def _(n):
        x = [
            jnp.concatenate([k_ref[8 * g + i, :, 128 * h : 128 * h + 128] for g in range(8)], 0) for i in range(8)
        ]
        ys = reordered(jnp.concatenate(x, 1), order_ref, n)
        for to in range(2):
            for g in range(8):
                for c in range(2):
                    first = 64 * g + 32 * to
                    row = pl.ds(pl.multiple_of(256 * to + (2 * n + c) * 32, 32), 32)
                    a_ref[g % 4, row, 256 * h + 128 * (g // 4) : 256 * h + 128 * (g // 4) + 128] = ys[
                        first : first + 32, 128 * c : 128 * c + 128
                    ].astype(BF16)


def put_shifts(t_ref, rows, v, series):
    col = pl.ds(v * 128, 128)
    for start, shifted in zip(rows, series):
        for q in range(8):
            row = pl.multiple_of(start + 16 * q, 16)
            t_ref[pl.ds(row, 16), col] = jnp.concatenate(shifted[2 * q : 2 * q + 2], 0).astype(BF16)


def later(lo, hi, s):
    if s == 0:
        return lo, hi
    lane = lane_of(lo.shape[0])
    a, b = pltpu.roll(lo, s, 1), pltpu.roll(hi, s, 1)
    return jnp.where(lane < s, 0.0, a), jnp.where(lane < s, a, b)


def earlier(lo, hi, s):
    if s == 0:
        return lo, hi
    lane = lane_of(lo.shape[0])
    a, b = pltpu.roll(lo, 128 - s, 1), pltpu.roll(hi, 128 - s, 1)
    return jnp.where(lane < 128 - s, a, b), jnp.where(lane < 128 - s, b, 0.0)


def forward_shifts(t_ref, g, v, lo, hi):
    pairs = [later(lo, hi, 8 * l) for l in range(16)]
    put_shifts(t_ref, (1024 + g * 128, g * 128), v, zip(*pairs))


def adjoint_shifts(t_ref, half, v, lo, hi):
    pairs = [earlier(lo, hi, 8 * l) for l in range(16)]
    put_shifts(t_ref, (half * 128, 256 + half * 128), v, zip(*pairs))


def folded(shift, lo_ref, hi_ref, start, stride, v):
    col = slice(128 * v, 128 * v + 128)
    lo = hi = None
    for c in range(8):
        row = pl.ds(start + stride * c, 8)
        a, b = shift(lo_ref[row, col], hi_ref[row, col], c)
        lo, hi = (a, b) if lo is None else (lo + a, hi + b)
    return lo, hi


def body(
    k_hbm, hist_hbm, noise_hbm, out_ref,
    k_ref, noise_ref, wide_ref, x_ref, order_ref, a1_ref, a2_ref, t1_ref, long_ref, short_ref, t2_ref, q0_ref, q1_ref,
    hb, ybuf, yrecv, zrecv, wall, gf, gmsg, grecv,
    load_sem, told, h_send, h_recv, c_send, c_recv, z_send, z_recv, w_send, w_recv, wc_send, wc_recv, g_send, g_recv,
):
    ms, mp = lax.axis_index("sensor"), lax.axis_index("param")
    zh, y, core = mp // 8, (mp // 2) % 4, mp % 2

    def sensor_at(s):
        return {"sensor": s, "param": mp}

    def param_at(z_, y_, core_):
        return {"sensor": ms, "param": z_ * 8 + y_ * 2 + core_}

    partner = param_at(zh, y, 1 - core)

    pltpu.make_async_copy(hist_hbm, hb.at[ms], load_sem.at[0]).start()
    k_loads = []
    for part in range(4):
        rows = pl.ds(16 * part, 16)
        k_loads.append(pltpu.make_async_copy(k_hbm.at[rows], k_ref.at[rows], load_sem.at[2 + part]))
        k_loads[-1].start()
    pltpu.make_async_copy(noise_hbm, noise_ref, load_sem.at[1]).start()

    barrier = pltpu.get_barrier_semaphore()
    peers = [sensor_at((ms + k) % 8) for k in range(1, 8)]
    peers += [partner]
    peers += [param_at(zh, (y + dy) % 4, core) for dy in range(1, 4)]
    beside = [param_at((zh + dz) % 4, y, core) for dz in (1, 3)]
    peers += beside
    for peer in peers:
        pl.semaphore_signal(barrier, inc=1, device_id=peer, device_id_type=MESH)

    fill_order(order_ref)
    pltpu.make_async_copy(hist_hbm, hb.at[ms], load_sem.at[0]).wait()
    pl.semaphore_wait(barrier, len(peers))
    for peer in beside:
        pl.semaphore_signal(told.at[0], inc=1, device_id=peer, device_id_type=MESH)

    def send(src, dst, send_sem, recv_sem, peer):
        copy = pltpu.make_async_remote_copy(
            src_ref=src, dst_ref=dst, send_sem=send_sem, recv_sem=recv_sem, device_id=peer, device_id_type=MESH
        )
        copy.start()
        return copy

    def arrive(dst, recv_sem):
        pltpu.make_async_remote_copy(
            src_ref=dst, dst_ref=dst, send_sem=recv_sem, recv_sem=recv_sem, device_id=partner, device_id_type=MESH
        ).wait_recv()

    def sent_off(src, send_sem):
        pltpu.make_async_remote_copy(
            src_ref=src, dst_ref=src, send_sem=send_sem, recv_sem=send_sem, device_id=partner, device_id_type=MESH
        ).wait_send()

    sent = []
    for dz, dx in ((1, 2), (1, 1), (1, 3), (0, 2), (1, 0), (0, 1), (0, 3)):
        peer = sensor_at((ms // 4 + dz) % 2 * 4 + (ms + dx) % 4)
        sent.append(send(hb.at[ms], hb.at[ms], h_send.at[4 * dz + dx], h_recv.at[ms], peer))

    def sensor_of(k):
        dz = jnp.where(k == 3, 1, k // 5)
        dx = jnp.where((k == 4) | (k == 7), 2, jnp.where((k == 1) | (k == 5), 1, jnp.where((k == 2) | (k == 6), 3, 0)))
        return (ms // 4 + dz) % 2 * 4 + (ms + dx) % 4

    def series_of(s):
        block = hb[s].astype(F32)
        for v in range(6):
            forward_shifts(t1_ref, s, v, block[8 * v : 8 * v + 8, :128], block[8 * v : 8 * v + 8, 128:])

    def series(k):
        s = sensor_of(k)
        arrive(hb.at[s], h_recv.at[s])
        series_of(s)

    series_of(ms)

    def tell():
        pl.semaphore_wait(told.at[0], 2)
        for peer in beside:
            pl.semaphore_signal(told.at[1], inc=1, device_id=peer, device_id_type=MESH)

    for part in range(4):
        k_loads[part].wait()

        @pl.loop(8 * part, 8 * part + 8)
        def _(step):
            for u in range(2):
                i = 2 * step + u
                for h in range(2):
                    wide_ref[h, pl.ds(pl.multiple_of(i * 72, 8), 64), :] = k_ref[i, :, 128 * h : 128 * h + 128].astype(F32)

    forward_taps(wide_ref, x_ref, order_ref, a1_ref, lambda step: series(step - 4), tell)

    pl.loop(4, 8)(series)

    def z_of(b):
        return (zh + jnp.where(b == 0, 2, jnp.where(b == 1, 1, jnp.where(b == 2, 3, 0)))) % 4

    def pass_on(b, dys):
        arrive(yrecv.at[b], c_recv.at[b])
        for dy in dys:
            to = (y + dy) % 4
            ybuf[b, 1, to] = ybuf[b, 1, to] + yrecv[b, to]
            send(
                ybuf.at[b, 1, to], zrecv.at[zh * 4 + y], z_send.at[b, dy], z_recv.at[zh * 4 + y],
                param_at(z_of(b), to, core),
            )

    @pl.loop(0, 4)
    def _(b):
        z = z_of(b)
        long_ref[...] = jnp.dot(a1_ref[z], t1_ref[...], preferred_element_type=F32)
        short_ref[...] = jnp.dot(a1_ref[z, :, :1024], t1_ref[1024:, :], preferred_element_type=F32)
        for half in range(2):
            mine = (half + core + 1) % 2
            for v in range(6):
                lo, hi = folded(later, short_ref, long_ref, 8 * half, 16, v)
                col = slice(128 * (v % 3), 128 * (v % 3) + 128)
                ybuf[b, mine, v // 3, :, col] = lo
                ybuf[b, mine, 2 + v // 3, :, col] = hi
        send(ybuf.at[b, 0], yrecv.at[b], c_send.at[b], c_recv.at[b], partner)

        @pl.when(b == 1)
        def _():
            pl.semaphore_wait(told.at[1], 2)

        @pl.when(b > 0)
        def _():
            pass_on(b - 1, (2, 1, 3, 0))

    pass_on(3, (2, 1, 3))

    adjoint_taps(k_ref, order_ref, a2_ref, 0)

    piece = ybuf[3, 1, y] + yrecv[3, y]
    for dz in (2, 1, 3, 0):
        for dy in range(4):
            if dz or dy:
                at = ((zh + dz) % 4) * 4 + (y + dy) % 4
                arrive(zrecv.at[at], z_recv.at[at])
                piece = piece + zrecv[at]

    pltpu.make_async_copy(noise_hbm, noise_ref, load_sem.at[1]).wait()
    group = core * 4 + zh
    noise = noise_ref[pl.ds(pl.multiple_of(8 * group, 8), 8), pl.ds(pl.multiple_of(128 * (y // 2), 128), 128)]
    tiles = [piece[:, 128 * k : 128 * k + 128] * noise for k in range(3)]
    tiles.append(jnp.zeros_like(noise))
    here = group * 4 + y
    wall[here] = jnp.concatenate(
        [jnp.concatenate(tiles[:2], 1), jnp.concatenate(tiles[2:], 1)], 0
    ).astype(BF16)
    for dz in (2, 1, 3, 0):
        for dy in (2, 1, 3, 0):
            if dz or dy:
                peer = param_at((zh + dz) % 4, (y + dy) % 4, core)
                sent.append(send(wall.at[here], wall.at[here], w_send.at[dz * 4 + dy], w_recv.at[zh * 4 + y], peer))

    adjoint_taps(k_ref, order_ref, a2_ref, 1)
    q0_ref[...] = jnp.zeros_like(q0_ref)
    q1_ref[...] = jnp.zeros_like(q1_ref)

    def weighted_shifts(half, z):
        pieces = [wall[(half * 4 + z) * 4 + y_].astype(F32) for y_ in range(4)]
        for v in range(6):
            row, col = 8 * (v % 3 // 2), 128 * (v % 3 % 2)
            lo, hi = [pieces[y_][row : row + 8, col : col + 128] for y_ in (v // 3, 2 + v // 3)]
            adjoint_shifts(t2_ref, half, v, lo, hi)

    def z_in(step):
        return (zh + jnp.where(step == 0, 0, jnp.where(step == 1, 1, jnp.where(step == 2, 3, 2)))) % 4

    def fetch(step):
        z = z_in(step)
        for dy in (1, 3, 2, 0):
            at = (y + dy) % 4

            @pl.when((step > 0) | (dy > 0))
            def _():
                arrive(wall.at[(core * 4 + z) * 4 + at], w_recv.at[z * 4 + at])

        block = wall.at[pl.ds((core * 4 + z) * 4, 4)]
        send(block, block, wc_send.at[z], wc_recv.at[z], partner)

    def other_half(z):
        arrive(wall.at[pl.ds(((1 - core) * 4 + z) * 4, 4)], wc_recv.at[z])
        weighted_shifts(1 - core, z)

    fetch(0)

    @pl.loop(0, 4)
    def _(step):
        z = z_in(step)
        weighted_shifts(core, z)

        @pl.when(step < 3)
        def _():
            fetch(step + 1)

        other_half(z)

        @pl.when(step < 3)
        def _():
            q0_ref[...] += jnp.dot(a2_ref[z], t2_ref[...], preferred_element_type=F32)
            q1_ref[...] += jnp.dot(a2_ref[z, :, :256], t2_ref[256:, :], preferred_element_type=F32)

    @pl.loop(0, 2)
    def _(part):
        z = z_in(3)
        to_half = (ms // 4 + 1 + part) % 2
        rows = pl.ds(pl.multiple_of(256 * to_half, 256), 256)
        q0_ref[rows, :] += jnp.dot(a2_ref[z, rows, :], t2_ref[...], preferred_element_type=F32)
        q1_ref[rows, :] += jnp.dot(a2_ref[z, rows, :256], t2_ref[256:, :], preferred_element_type=F32)

        @pl.loop(0, 4)
        def _(turn):
            k = jnp.where(turn == 0, 2, jnp.where(turn == 1, 1, jnp.where(turn == 2, 3, 0)))
            r = (ms + k) % 4
            slot = to_half * 4 + r
            for v in range(6):
                lo, hi = folded(earlier, q0_ref, q1_ref, pl.multiple_of(256 * to_half + 8 * r, 8), 32, v)
                both = jnp.concatenate([lo, hi], 0)
                gf[:, 128 * v : 128 * v + 128] = both
                gmsg[slot, :, 128 * v : 128 * v + 128] = both.astype(BF16)

            @pl.when((part == 0) | (turn < 3))
            def _():
                send(gmsg.at[slot], grecv.at[ms], g_send.at[slot], g_recv.at[ms], sensor_at(slot))

    total = gf[...]
    for k in (1, 3, 2):
        at = (ms // 4) * 4 + (ms + k) % 4
        arrive(grecv.at[at], g_recv.at[at])
        total = total + grecv[at].astype(F32)
    for k in range(4):
        at = (1 - ms // 4) * 4 + (ms + k) % 4
        arrive(grecv.at[at], g_recv.at[at])
        total = total + grecv[at].astype(F32)
    for v in range(6):
        for t in range(2):
            out_ref[8 * v : 8 * v + 8, 128 * t : 128 * t + 128] = total[8 * t : 8 * t + 8, 128 * v : 128 * v + 128]

    for copy in sent:
        copy.wait_send()
    for k in range(1, 8):
        slot = (ms + k) % 8
        sent_off(gmsg.at[slot], g_send.at[slot])

    @pl.loop(0, 4)
    def _(b):
        sent_off(ybuf.at[b, 0], c_send.at[b])
        sent_off(wall.at[pl.ds((core * 4 + b) * 4, 4)], wc_send.at[b])
        for dy in range(4):

            @pl.when((b < 3) | (dy > 0))
            def _():
                sent_off(ybuf.at[b, 1, (y + dy) % 4], z_send.at[b, dy])


def shards(histories, kernel, noise_weight):
    V, S = pltpu.VMEM, pltpu.SemaphoreType.DMA
    out = pl.pallas_call(
        body,
        out_shape=jax.ShapeDtypeStruct((48, 256), F32),
        in_specs=[pl.BlockSpec(memory_space=pltpu.HBM)] * 3,
        out_specs=pl.BlockSpec(memory_space=pltpu.VMEM),
        scratch_shapes=[
            V((64, 64, 256), BF16), V((64, 256), F32), V((2, 4608, 128), F32), V((2, 512, 1024), BF16),
            V((1024, 1024), BF16), V((4, 128, 2048), BF16), V((4, 512, 512), BF16), V((2048, 768), BF16),
            V((128, 768), F32), V((128, 768), F32), V((512, 768), BF16), V((512, 768), F32), V((512, 768), F32),
            V((8, 48, 256), BF16), V((4, 2, 4, 8, 384), F32), V((4, 4, 8, 384), F32), V((16, 8, 384), F32),
            V((32, 16, 256), BF16), V((16, 768), F32), V((8, 16, 768), BF16), V((8, 16, 768), BF16),
            S((6,)), pltpu.SemaphoreType.REGULAR((2,)), S((8,)), S((8,)), S((4,)), S((4,)), S((4, 4)), S((16,)), S((16,)), S((16,)), S((4,)), S((4,)),
            S((8,)), S((8,)),
        ],
        compiler_params=pltpu.CompilerParams(
            collective_id=0, has_side_effects=True, vmem_limit_bytes=60 * 2**20
        ),
        cost_estimate=pl.CostEstimate(flops=4831838208, bytes_accessed=2300000, transcendentals=0),
        name="hessian",
    )(kernel, histories.transpose(1, 0, 2).reshape(48, 256), noise_weight)
    return out.reshape(6, 8, 256).transpose(1, 0, 2)


def solution(mesh):
    in_specs = (P(("param", "sensor"), None, None), P("sensor", "param", None), P("sensor", None))
    out_specs = P(("param", "sensor"), None, None)
    return jax.shard_map(shards, mesh=mesh, in_specs=in_specs, out_specs=out_specs, check_vma=False)
```

```python
import jax
import jax.numpy as jnp
from jax import lax
from jax.experimental import pallas as pl
from jax.experimental.pallas import tpu as pltpu
from jax.sharding import PartitionSpec as P

F32, BF16 = jnp.float32, jnp.bfloat16
MESH = pl.DeviceIdType.MESH


def lane_of(rows):
    return lax.broadcasted_iota(jnp.int32, (rows, 128), 1)


def fill_order(order_ref):
    row, col = [lax.broadcasted_iota(jnp.int32, (128, 1024), d) for d in (0, 1)]
    low = row & 7
    target = low * 128 + (row - low)

    @pl.loop(0, 8)
    def _(j):
        here = jnp.where(col == target + j, 1.0, 0.0).astype(BF16)
        order_ref[pl.ds(pl.multiple_of(j * 128, 128), 128), :] = here


def reordered(x, order_ref, n):
    return jnp.dot(x, order_ref[:, pl.ds(pl.multiple_of(n * 256, 256), 256)], preferred_element_type=F32)


def forward_taps(wide_ref, x_ref, order_ref, a_ref, beside, tell):
    for h in range(2):

        @pl.loop(0, 8)
        def _(g):
            row = pl.ds(pl.multiple_of(64 * g, 64), 64)
            for j in range(8):
                x_ref[h, row, 128 * j : 128 * j + 128] = wide_ref[h, pl.ds(8 * g + j, 64, stride=72), :].astype(BF16)

    def one(step):
        h, n = step // 4, step % 4
        ys = reordered(x_ref[h], order_ref, n)
        for z in range(4):
            for g in range(8):
                for c in range(2):
                    first = 64 * g + 8 * z
                    part = [ys[r : r + 8, 128 * c : 128 * c + 128] for r in (first, first + 32)]
                    row = pl.ds(pl.multiple_of((2 * n + c) * 16, 16), 16)
                    col = pl.ds(pl.multiple_of(h * 1024 + g * 128, 128), 128)
                    a_ref[z, row, col] = jnp.concatenate(part, 0).astype(BF16)

    pl.loop(0, 5)(one)
    tell()

    @pl.loop(5, 8)
    def _(step):
        beside(step)
        one(step)


def adjoint_taps(k_ref, order_ref, a_ref, h):
    @pl.loop(0, 4)
    def _(n):
        x = [
            jnp.concatenate([k_ref[8 * g + i, :, 128 * h : 128 * h + 128] for g in range(8)], 0) for i in range(8)
        ]
        ys = reordered(jnp.concatenate(x, 1), order_ref, n)
        for to in range(2):
            for g in range(8):
                for c in range(2):
                    first = 64 * g + 32 * to
                    row = pl.ds(pl.multiple_of(256 * to + (2 * n + c) * 32, 32), 32)
                    a_ref[g % 4, row, 256 * h + 128 * (g // 4) : 256 * h + 128 * (g // 4) + 128] = ys[
                        first : first + 32, 128 * c : 128 * c + 128
                    ].astype(BF16)


def put_shifts(t_ref, rows, v, series):
    col = pl.ds(v * 128, 128)
    for start, shifted in zip(rows, series):
        for q in range(8):
            row = pl.multiple_of(start + 16 * q, 16)
            t_ref[pl.ds(row, 16), col] = jnp.concatenate(shifted[2 * q : 2 * q + 2], 0).astype(BF16)


def later(lo, hi, s):
    if s == 0:
        return lo, hi
    lane = lane_of(lo.shape[0])
    a, b = pltpu.roll(lo, s, 1), pltpu.roll(hi, s, 1)
    return jnp.where(lane < s, 0.0, a), jnp.where(lane < s, a, b)


def earlier(lo, hi, s):
    if s == 0:
        return lo, hi
    lane = lane_of(lo.shape[0])
    a, b = pltpu.roll(lo, 128 - s, 1), pltpu.roll(hi, 128 - s, 1)
    return jnp.where(lane < 128 - s, a, b), jnp.where(lane < 128 - s, b, 0.0)


def forward_shifts(t_ref, g, v, lo, hi):
    pairs = [later(lo, hi, 8 * l) for l in range(16)]
    put_shifts(t_ref, (1024 + g * 128, g * 128), v, zip(*pairs))


def adjoint_shifts(t_ref, half, v, lo, hi):
    pairs = [earlier(lo, hi, 8 * l) for l in range(16)]
    put_shifts(t_ref, (half * 128, 256 + half * 128), v, zip(*pairs))


def folded(shift, lo_ref, hi_ref, start, stride, v):
    col = slice(128 * v, 128 * v + 128)
    lo = hi = None
    for c in range(8):
        row = pl.ds(start + stride * c, 8)
        a, b = shift(lo_ref[row, col], hi_ref[row, col], c)
        lo, hi = (a, b) if lo is None else (lo + a, hi + b)
    return lo, hi


def body(
    k_hbm, hist_hbm, noise_hbm, out_ref,
    k_ref, noise_ref, wide_ref, x_ref, order_ref, a1_ref, a2_ref, t1_ref, long_ref, short_ref, t2_ref, q0_ref, q1_ref,
    hb, ybuf, yrecv, zrecv, wall, gf, gmsg, grecv,
    load_sem, told, h_send, h_recv, c_send, c_recv, z_send, z_recv, w_send, w_recv, wc_send, wc_recv, g_send, g_recv,
):
    ms, mp = lax.axis_index("sensor"), lax.axis_index("param")
    zh, y, core = mp // 8, (mp // 2) % 4, mp % 2

    def sensor_at(s):
        return {"sensor": s, "param": mp}

    def param_at(z_, y_, core_):
        return {"sensor": ms, "param": z_ * 8 + y_ * 2 + core_}

    partner = param_at(zh, y, 1 - core)

    pltpu.make_async_copy(hist_hbm, hb.at[ms], load_sem.at[0]).start()
    k_loads = []
    for part in range(4):
        rows = pl.ds(16 * part, 16)
        k_loads.append(pltpu.make_async_copy(k_hbm.at[rows], k_ref.at[rows], load_sem.at[2 + part]))
        k_loads[-1].start()
    pltpu.make_async_copy(noise_hbm, noise_ref, load_sem.at[1]).start()

    barrier = pltpu.get_barrier_semaphore()
    peers = [sensor_at((ms + k) % 8) for k in range(1, 8)]
    peers += [partner]
    peers += [param_at(zh, (y + dy) % 4, core) for dy in range(1, 4)]
    beside = [param_at((zh + dz) % 4, y, core) for dz in (1, 3)]
    peers += beside
    for peer in peers:
        pl.semaphore_signal(barrier, inc=1, device_id=peer, device_id_type=MESH)

    fill_order(order_ref)
    pltpu.make_async_copy(hist_hbm, hb.at[ms], load_sem.at[0]).wait()
    pl.semaphore_wait(barrier, len(peers))
    for peer in beside:
        pl.semaphore_signal(told.at[0], inc=1, device_id=peer, device_id_type=MESH)

    def send(src, dst, send_sem, recv_sem, peer):
        copy = pltpu.make_async_remote_copy(
            src_ref=src, dst_ref=dst, send_sem=send_sem, recv_sem=recv_sem, device_id=peer, device_id_type=MESH
        )
        copy.start()
        return copy

    def arrive(dst, recv_sem):
        pltpu.make_async_remote_copy(
            src_ref=dst, dst_ref=dst, send_sem=recv_sem, recv_sem=recv_sem, device_id=partner, device_id_type=MESH
        ).wait_recv()

    def sent_off(src, send_sem):
        pltpu.make_async_remote_copy(
            src_ref=src, dst_ref=src, send_sem=send_sem, recv_sem=send_sem, device_id=partner, device_id_type=MESH
        ).wait_send()

    sent = []
    for dz, dx in ((1, 2), (1, 1), (1, 3), (0, 2), (1, 0), (0, 1), (0, 3)):
        peer = sensor_at((ms // 4 + dz) % 2 * 4 + (ms + dx) % 4)
        sent.append(send(hb.at[ms], hb.at[ms], h_send.at[4 * dz + dx], h_recv.at[ms], peer))

    def sensor_of(k):
        dz = jnp.where(k == 3, 1, k // 5)
        dx = jnp.where((k == 4) | (k == 7), 2, jnp.where((k == 1) | (k == 5), 1, jnp.where((k == 2) | (k == 6), 3, 0)))
        return (ms // 4 + dz) % 2 * 4 + (ms + dx) % 4

    def series_of(s):
        block = hb[s].astype(F32)
        for v in range(6):
            forward_shifts(t1_ref, s, v, block[8 * v : 8 * v + 8, :128], block[8 * v : 8 * v + 8, 128:])

    def series(k):
        s = sensor_of(k)
        arrive(hb.at[s], h_recv.at[s])
        series_of(s)

    series_of(ms)

    def tell():
        pl.semaphore_wait(told.at[0], 2)
        for peer in beside:
            pl.semaphore_signal(told.at[1], inc=1, device_id=peer, device_id_type=MESH)

    for part in range(4):
        k_loads[part].wait()

        @pl.loop(8 * part, 8 * part + 8)
        def _(step):
            for u in range(2):
                i = 2 * step + u
                for h in range(2):
                    wide_ref[h, pl.ds(pl.multiple_of(i * 72, 8), 64), :] = k_ref[i, :, 128 * h : 128 * h + 128].astype(F32)

    forward_taps(wide_ref, x_ref, order_ref, a1_ref, lambda step: series(step - 4), tell)

    pl.loop(4, 8)(series)

    def z_of(b):
        return (zh + jnp.where(b == 0, 2, jnp.where(b == 1, 1, jnp.where(b == 2, 3, 0)))) % 4

    def pass_on(b, dys):
        arrive(yrecv.at[b], c_recv.at[b])
        for dy in dys:
            to = (y + dy) % 4
            ybuf[b, 1, to] = ybuf[b, 1, to] + yrecv[b, to]
            send(
                ybuf.at[b, 1, to], zrecv.at[zh * 4 + y], z_send.at[b, dy], z_recv.at[zh * 4 + y],
                param_at(z_of(b), to, core),
            )

    @pl.loop(0, 4)
    def _(b):
        z = z_of(b)
        long_ref[...] = jnp.dot(a1_ref[z], t1_ref[...], preferred_element_type=F32)
        short_ref[...] = jnp.dot(a1_ref[z, :, :1024], t1_ref[1024:, :], preferred_element_type=F32)
        for half in range(2):
            mine = (half + core + 1) % 2
            for v in range(6):
                lo, hi = folded(later, short_ref, long_ref, 8 * half, 16, v)
                col = slice(128 * (v % 3), 128 * (v % 3) + 128)
                ybuf[b, mine, v // 3, :, col] = lo
                ybuf[b, mine, 2 + v // 3, :, col] = hi
        send(ybuf.at[b, 0], yrecv.at[b], c_send.at[b], c_recv.at[b], partner)

        @pl.when(b == 1)
        def _():
            pl.semaphore_wait(told.at[1], 2)

        @pl.when(b > 0)
        def _():
            pass_on(b - 1, (2, 1, 3, 0))

    pass_on(3, (2, 1, 3))

    adjoint_taps(k_ref, order_ref, a2_ref, 0)

    piece = ybuf[3, 1, y] + yrecv[3, y]
    for dz in (2, 1, 3, 0):
        for dy in range(4):
            if dz or dy:
                at = ((zh + dz) % 4) * 4 + (y + dy) % 4
                arrive(zrecv.at[at], z_recv.at[at])
                piece = piece + zrecv[at]

    pltpu.make_async_copy(noise_hbm, noise_ref, load_sem.at[1]).wait()
    group = core * 4 + zh
    noise = noise_ref[pl.ds(pl.multiple_of(8 * group, 8), 8), pl.ds(pl.multiple_of(128 * (y // 2), 128), 128)]
    tiles = [piece[:, 128 * k : 128 * k + 128] * noise for k in range(3)]
    tiles.append(jnp.zeros_like(noise))
    here = group * 4 + y
    wall[here] = jnp.concatenate(
        [jnp.concatenate(tiles[:2], 1), jnp.concatenate(tiles[2:], 1)], 0
    ).astype(BF16)
    for dz in (0, 2, 1, 3):
        for dy in (2, 1, 3, 0):
            if dz or dy:
                peer = param_at((zh + dz) % 4, (y + dy) % 4, core)
                sent.append(send(wall.at[here], wall.at[here], w_send.at[dz * 4 + dy], w_recv.at[zh * 4 + y], peer))

    adjoint_taps(k_ref, order_ref, a2_ref, 1)
    q0_ref[...] = jnp.zeros_like(q0_ref)
    q1_ref[...] = jnp.zeros_like(q1_ref)

    def weighted_shifts(half, z):
        pieces = [wall[(half * 4 + z) * 4 + y_].astype(F32) for y_ in range(4)]
        for v in range(6):
            row, col = 8 * (v % 3 // 2), 128 * (v % 3 % 2)
            lo, hi = [pieces[y_][row : row + 8, col : col + 128] for y_ in (v // 3, 2 + v // 3)]
            adjoint_shifts(t2_ref, half, v, lo, hi)

    def z_in(step):
        return (zh + jnp.where(step == 0, 0, jnp.where(step == 1, 1, jnp.where(step == 2, 3, 2)))) % 4

    def fetch(step):
        z = z_in(step)
        for dy in (1, 3, 2, 0):
            at = (y + dy) % 4

            @pl.when((step > 0) | (dy > 0))
            def _():
                arrive(wall.at[(core * 4 + z) * 4 + at], w_recv.at[z * 4 + at])

        block = wall.at[pl.ds((core * 4 + z) * 4, 4)]
        send(block, block, wc_send.at[z], wc_recv.at[z], partner)

    def other_half(z):
        arrive(wall.at[pl.ds(((1 - core) * 4 + z) * 4, 4)], wc_recv.at[z])
        weighted_shifts(1 - core, z)

    fetch(0)

    @pl.loop(0, 4)
    def _(step):
        z = z_in(step)
        weighted_shifts(core, z)

        @pl.when(step < 3)
        def _():
            fetch(step + 1)

        other_half(z)

        @pl.when(step < 3)
        def _():
            q0_ref[...] += jnp.dot(a2_ref[z], t2_ref[...], preferred_element_type=F32)
            q1_ref[...] += jnp.dot(a2_ref[z, :, :256], t2_ref[256:, :], preferred_element_type=F32)

    @pl.loop(0, 2)
    def _(part):
        z = z_in(3)
        to_half = (ms // 4 + 1 + part) % 2
        rows = pl.ds(pl.multiple_of(256 * to_half, 256), 256)
        q0_ref[rows, :] += jnp.dot(a2_ref[z, rows, :], t2_ref[...], preferred_element_type=F32)
        q1_ref[rows, :] += jnp.dot(a2_ref[z, rows, :256], t2_ref[256:, :], preferred_element_type=F32)

        @pl.loop(0, 4)
        def _(turn):
            k = jnp.where(turn == 0, 2, jnp.where(turn == 1, 1, jnp.where(turn == 2, 3, 0)))
            r = (ms + k) % 4
            slot = to_half * 4 + r
            for v in range(6):
                lo, hi = folded(earlier, q0_ref, q1_ref, pl.multiple_of(256 * to_half + 8 * r, 8), 32, v)
                both = jnp.concatenate([lo, hi], 0)
                gf[:, 128 * v : 128 * v + 128] = both
                gmsg[slot, :, 128 * v : 128 * v + 128] = both.astype(BF16)

            @pl.when((part == 0) | (turn < 3))
            def _():
                send(gmsg.at[slot], grecv.at[ms], g_send.at[slot], g_recv.at[ms], sensor_at(slot))

    total = gf[...]
    for k in (1, 3, 2):
        at = (ms // 4) * 4 + (ms + k) % 4
        arrive(grecv.at[at], g_recv.at[at])
        total = total + grecv[at].astype(F32)
    for k in range(4):
        at = (1 - ms // 4) * 4 + (ms + k) % 4
        arrive(grecv.at[at], g_recv.at[at])
        total = total + grecv[at].astype(F32)
    for v in range(6):
        for t in range(2):
            out_ref[8 * v : 8 * v + 8, 128 * t : 128 * t + 128] = total[8 * t : 8 * t + 8, 128 * v : 128 * v + 128]

    for copy in sent:
        copy.wait_send()
    for k in range(1, 8):
        slot = (ms + k) % 8
        sent_off(gmsg.at[slot], g_send.at[slot])

    @pl.loop(0, 4)
    def _(b):
        sent_off(ybuf.at[b, 0], c_send.at[b])
        sent_off(wall.at[pl.ds((core * 4 + b) * 4, 4)], wc_send.at[b])
        for dy in range(4):

            @pl.when((b < 3) | (dy > 0))
            def _():
                sent_off(ybuf.at[b, 1, (y + dy) % 4], z_send.at[b, dy])


def shards(histories, kernel, noise_weight):
    V, S = pltpu.VMEM, pltpu.SemaphoreType.DMA
    out = pl.pallas_call(
        body,
        out_shape=jax.ShapeDtypeStruct((48, 256), F32),
        in_specs=[pl.BlockSpec(memory_space=pltpu.HBM)] * 3,
        out_specs=pl.BlockSpec(memory_space=pltpu.VMEM),
        scratch_shapes=[
            V((64, 64, 256), BF16), V((64, 256), F32), V((2, 4608, 128), F32), V((2, 512, 1024), BF16),
            V((1024, 1024), BF16), V((4, 128, 2048), BF16), V((4, 512, 512), BF16), V((2048, 768), BF16),
            V((128, 768), F32), V((128, 768), F32), V((512, 768), BF16), V((512, 768), F32), V((512, 768), F32),
            V((8, 48, 256), BF16), V((4, 2, 4, 8, 384), F32), V((4, 4, 8, 384), F32), V((16, 8, 384), F32),
            V((32, 16, 256), BF16), V((16, 768), F32), V((8, 16, 768), BF16), V((8, 16, 768), BF16),
            S((6,)), pltpu.SemaphoreType.REGULAR((2,)), S((8,)), S((8,)), S((4,)), S((4,)), S((4, 4)), S((16,)), S((16,)), S((16,)), S((4,)), S((4,)),
            S((8,)), S((8,)),
        ],
        compiler_params=pltpu.CompilerParams(
            collective_id=0, has_side_effects=True, vmem_limit_bytes=60 * 2**20
        ),
        cost_estimate=pl.CostEstimate(flops=4831838208, bytes_accessed=2300000, transcendentals=0),
        name="hessian",
    )(kernel, histories.transpose(1, 0, 2).reshape(48, 256), noise_weight)
    return out.reshape(6, 8, 256).transpose(1, 0, 2)


def solution(mesh):
    in_specs = (P(("param", "sensor"), None, None), P("sensor", "param", None), P("sensor", None))
    out_specs = P(("param", "sensor"), None, None)
    return jax.shard_map(shards, mesh=mesh, in_specs=in_specs, out_specs=out_specs, check_vma=False)
```

```python
import jax
import jax.numpy as jnp
from jax import lax
from jax.experimental import pallas as pl
from jax.experimental.pallas import tpu as pltpu
from jax.sharding import PartitionSpec as P

F32, BF16 = jnp.float32, jnp.bfloat16
MESH = pl.DeviceIdType.MESH


def lane_of(rows):
    return lax.broadcasted_iota(jnp.int32, (rows, 128), 1)


def fill_order(order_ref):
    row, col = [lax.broadcasted_iota(jnp.int32, (128, 1024), d) for d in (0, 1)]
    low = row & 7
    target = low * 128 + (row - low)

    @pl.loop(0, 8)
    def _(j):
        here = jnp.where(col == target + j, 1.0, 0.0).astype(BF16)
        order_ref[pl.ds(pl.multiple_of(j * 128, 128), 128), :] = here


def reordered(x, order_ref, n):
    return jnp.dot(x, order_ref[:, pl.ds(pl.multiple_of(n * 256, 256), 256)], preferred_element_type=F32)


def group_taps(wide_ref, x_ref):
    for h in range(2):

        @pl.loop(0, 8)
        def _(g):
            row = pl.ds(pl.multiple_of(64 * g, 64), 64)
            for j in range(8):
                x_ref[h, row, 128 * j : 128 * j + 128] = wide_ref[h, pl.ds(8 * g + j, 64, stride=72), :].astype(BF16)


def forward_taps(wide_ref, x_ref, order_ref, a_ref, beside, tell):
    def one(step):
        h, n = step // 4, step % 4
        ys = reordered(x_ref[h], order_ref, n)
        for z in range(4):
            for g in range(8):
                for c in range(2):
                    first = 64 * g + 8 * z
                    part = [ys[r : r + 8, 128 * c : 128 * c + 128] for r in (first, first + 32)]
                    row = pl.ds(pl.multiple_of((2 * n + c) * 16, 16), 16)
                    col = pl.ds(pl.multiple_of(h * 1024 + g * 128, 128), 128)
                    a_ref[z, row, col] = jnp.concatenate(part, 0).astype(BF16)

    pl.loop(0, 5)(one)
    tell()

    @pl.loop(5, 8)
    def _(step):
        beside(step)
        one(step)


def adjoint_taps(k_ref, order_ref, a_ref, h):
    @pl.loop(0, 4)
    def _(n):
        x = [
            jnp.concatenate([k_ref[8 * g + i, :, 128 * h : 128 * h + 128] for g in range(8)], 0) for i in range(8)
        ]
        ys = reordered(jnp.concatenate(x, 1), order_ref, n)
        for to in range(2):
            for g in range(8):
                for c in range(2):
                    first = 64 * g + 32 * to
                    row = pl.ds(pl.multiple_of(256 * to + (2 * n + c) * 32, 32), 32)
                    a_ref[g % 4, row, 256 * h + 128 * (g // 4) : 256 * h + 128 * (g // 4) + 128] = ys[
                        first : first + 32, 128 * c : 128 * c + 128
                    ].astype(BF16)


def put_shifts(t_ref, rows, v, series):
    col = pl.ds(v * 128, 128)
    for start, shifted in zip(rows, series):
        for q in range(8):
            row = pl.multiple_of(start + 16 * q, 16)
            t_ref[pl.ds(row, 16), col] = jnp.concatenate(shifted[2 * q : 2 * q + 2], 0).astype(BF16)


def later(lo, hi, s):
    if s == 0:
        return lo, hi
    lane = lane_of(lo.shape[0])
    a, b = pltpu.roll(lo, s, 1), pltpu.roll(hi, s, 1)
    return jnp.where(lane < s, 0.0, a), jnp.where(lane < s, a, b)


def earlier(lo, hi, s):
    if s == 0:
        return lo, hi
    lane = lane_of(lo.shape[0])
    a, b = pltpu.roll(lo, 128 - s, 1), pltpu.roll(hi, 128 - s, 1)
    return jnp.where(lane < 128 - s, a, b), jnp.where(lane < 128 - s, b, 0.0)


def forward_shifts(t_ref, g, v, lo, hi):
    pairs = [later(lo, hi, 8 * l) for l in range(16)]
    put_shifts(t_ref, (1024 + g * 128, g * 128), v, zip(*pairs))


def adjoint_shifts(t_ref, half, v, lo, hi):
    pairs = [earlier(lo, hi, 8 * l) for l in range(16)]
    put_shifts(t_ref, (half * 128, 256 + half * 128), v, zip(*pairs))


def folded(shift, lo_ref, hi_ref, start, stride, v):
    col = slice(128 * v, 128 * v + 128)
    lo = hi = None
    for c in range(8):
        row = pl.ds(start + stride * c, 8)
        a, b = shift(lo_ref[row, col], hi_ref[row, col], c)
        lo, hi = (a, b) if lo is None else (lo + a, hi + b)
    return lo, hi


def body(
    k_hbm, hist_hbm, noise_hbm, out_ref,
    k_ref, noise_ref, wide_ref, x_ref, order_ref, a1_ref, a2_ref, t1_ref, long_ref, short_ref, t2_ref, q0_ref, q1_ref,
    hb, ybuf, yrecv, zrecv, wall, gf, gmsg, grecv,
    load_sem, told, h_send, h_recv, c_send, c_recv, z_send, z_recv, w_send, w_recv, wc_send, wc_recv, g_send, g_recv,
):
    ms, mp = lax.axis_index("sensor"), lax.axis_index("param")
    zh, y, core = mp // 8, (mp // 2) % 4, mp % 2

    def sensor_at(s):
        return {"sensor": s, "param": mp}

    def param_at(z_, y_, core_):
        return {"sensor": ms, "param": z_ * 8 + y_ * 2 + core_}

    partner = param_at(zh, y, 1 - core)

    pltpu.make_async_copy(hist_hbm, hb.at[ms], load_sem.at[0]).start()
    k_loads = []
    for part in range(4):
        rows = pl.ds(16 * part, 16)
        k_loads.append(pltpu.make_async_copy(k_hbm.at[rows], k_ref.at[rows], load_sem.at[2 + part]))
        k_loads[-1].start()
    pltpu.make_async_copy(noise_hbm, noise_ref, load_sem.at[1]).start()

    barrier = pltpu.get_barrier_semaphore()
    peers = [sensor_at((ms + k) % 8) for k in range(1, 8)]
    peers += [partner]
    peers += [param_at(zh, (y + dy) % 4, core) for dy in range(1, 4)]
    beside = [param_at((zh + dz) % 4, y, core) for dz in (1, 3)]
    peers += beside
    for peer in peers:
        pl.semaphore_signal(barrier, inc=1, device_id=peer, device_id_type=MESH)

    fill_order(order_ref)
    for part in range(4):
        k_loads[part].wait()

        @pl.loop(8 * part, 8 * part + 8)
        def _(step):
            for u in range(2):
                i = 2 * step + u
                for h in range(2):
                    wide_ref[h, pl.ds(pl.multiple_of(i * 72, 8), 64), :] = k_ref[i, :, 128 * h : 128 * h + 128].astype(F32)

    group_taps(wide_ref, x_ref)
    pltpu.make_async_copy(hist_hbm, hb.at[ms], load_sem.at[0]).wait()
    pl.semaphore_wait(barrier, len(peers))
    for peer in beside:
        pl.semaphore_signal(told.at[0], inc=1, device_id=peer, device_id_type=MESH)

    def send(src, dst, send_sem, recv_sem, peer):
        copy = pltpu.make_async_remote_copy(
            src_ref=src, dst_ref=dst, send_sem=send_sem, recv_sem=recv_sem, device_id=peer, device_id_type=MESH
        )
        copy.start()
        return copy

    def arrive(dst, recv_sem):
        pltpu.make_async_remote_copy(
            src_ref=dst, dst_ref=dst, send_sem=recv_sem, recv_sem=recv_sem, device_id=partner, device_id_type=MESH
        ).wait_recv()

    def sent_off(src, send_sem):
        pltpu.make_async_remote_copy(
            src_ref=src, dst_ref=src, send_sem=send_sem, recv_sem=send_sem, device_id=partner, device_id_type=MESH
        ).wait_send()

    sent = []
    for dz, dx in ((1, 2), (1, 1), (1, 3), (0, 2), (1, 0), (0, 1), (0, 3)):
        peer = sensor_at((ms // 4 + dz) % 2 * 4 + (ms + dx) % 4)
        sent.append(send(hb.at[ms], hb.at[ms], h_send.at[4 * dz + dx], h_recv.at[ms], peer))

    def sensor_of(k):
        dz = jnp.where(k == 3, 1, k // 5)
        dx = jnp.where((k == 4) | (k == 7), 2, jnp.where((k == 1) | (k == 5), 1, jnp.where((k == 2) | (k == 6), 3, 0)))
        return (ms // 4 + dz) % 2 * 4 + (ms + dx) % 4

    def series_of(s):
        block = hb[s].astype(F32)
        for v in range(6):
            forward_shifts(t1_ref, s, v, block[8 * v : 8 * v + 8, :128], block[8 * v : 8 * v + 8, 128:])

    def series(k):
        s = sensor_of(k)
        arrive(hb.at[s], h_recv.at[s])
        series_of(s)

    series_of(ms)

    def tell():
        pl.semaphore_wait(told.at[0], 2)
        for peer in beside:
            pl.semaphore_signal(told.at[1], inc=1, device_id=peer, device_id_type=MESH)

    forward_taps(wide_ref, x_ref, order_ref, a1_ref, lambda step: series(step - 4), tell)

    pl.loop(4, 8)(series)

    def z_of(b):
        return (zh + jnp.where(b == 0, 2, jnp.where(b == 1, 1, jnp.where(b == 2, 3, 0)))) % 4

    def pass_on(b, dys):
        arrive(yrecv.at[b], c_recv.at[b])
        for dy in dys:
            to = (y + dy) % 4
            ybuf[b, 1, to] = ybuf[b, 1, to] + yrecv[b, to]
            send(
                ybuf.at[b, 1, to], zrecv.at[zh * 4 + y], z_send.at[b, dy], z_recv.at[zh * 4 + y],
                param_at(z_of(b), to, core),
            )

    @pl.loop(0, 4)
    def _(b):
        z = z_of(b)
        long_ref[...] = jnp.dot(a1_ref[z], t1_ref[...], preferred_element_type=F32)
        short_ref[...] = jnp.dot(a1_ref[z, :, :1024], t1_ref[1024:, :], preferred_element_type=F32)
        for half in range(2):
            mine = (half + core + 1) % 2
            for v in range(6):
                lo, hi = folded(later, short_ref, long_ref, 8 * half, 16, v)
                col = slice(128 * (v % 3), 128 * (v % 3) + 128)
                ybuf[b, mine, v // 3, :, col] = lo
                ybuf[b, mine, 2 + v // 3, :, col] = hi
        send(ybuf.at[b, 0], yrecv.at[b], c_send.at[b], c_recv.at[b], partner)

        @pl.when(b == 1)
        def _():
            pl.semaphore_wait(told.at[1], 2)

        @pl.when(b > 0)
        def _():
            pass_on(b - 1, (2, 1, 3, 0))

    pass_on(3, (2, 1, 3))

    adjoint_taps(k_ref, order_ref, a2_ref, 0)

    piece = ybuf[3, 1, y] + yrecv[3, y]
    for dz in (2, 1, 3, 0):
        for dy in range(4):
            if dz or dy:
                at = ((zh + dz) % 4) * 4 + (y + dy) % 4
                arrive(zrecv.at[at], z_recv.at[at])
                piece = piece + zrecv[at]

    pltpu.make_async_copy(noise_hbm, noise_ref, load_sem.at[1]).wait()
    group = core * 4 + zh
    noise = noise_ref[pl.ds(pl.multiple_of(8 * group, 8), 8), pl.ds(pl.multiple_of(128 * (y // 2), 128), 128)]
    tiles = [piece[:, 128 * k : 128 * k + 128] * noise for k in range(3)]
    tiles.append(jnp.zeros_like(noise))
    here = group * 4 + y
    wall[here] = jnp.concatenate(
        [jnp.concatenate(tiles[:2], 1), jnp.concatenate(tiles[2:], 1)], 0
    ).astype(BF16)
    for dz in (2, 1, 3, 0):
        for dy in (2, 1, 3, 0):
            if dz or dy:
                peer = param_at((zh + dz) % 4, (y + dy) % 4, core)
                sent.append(send(wall.at[here], wall.at[here], w_send.at[dz * 4 + dy], w_recv.at[zh * 4 + y], peer))

    adjoint_taps(k_ref, order_ref, a2_ref, 1)
    q0_ref[...] = jnp.zeros_like(q0_ref)
    q1_ref[...] = jnp.zeros_like(q1_ref)

    def weighted_shifts(half, z):
        pieces = [wall[(half * 4 + z) * 4 + y_].astype(F32) for y_ in range(4)]
        for v in range(6):
            row, col = 8 * (v % 3 // 2), 128 * (v % 3 % 2)
            lo, hi = [pieces[y_][row : row + 8, col : col + 128] for y_ in (v // 3, 2 + v // 3)]
            adjoint_shifts(t2_ref, half, v, lo, hi)

    def z_in(step):
        return (zh + jnp.where(step == 0, 0, jnp.where(step == 1, 1, jnp.where(step == 2, 3, 2)))) % 4

    def fetch(step):
        z = z_in(step)
        for dy in (1, 3, 2, 0):
            at = (y + dy) % 4

            @pl.when((step > 0) | (dy > 0))
            def _():
                arrive(wall.at[(core * 4 + z) * 4 + at], w_recv.at[z * 4 + at])

        block = wall.at[pl.ds((core * 4 + z) * 4, 4)]
        send(block, block, wc_send.at[z], wc_recv.at[z], partner)

    def other_half(z):
        arrive(wall.at[pl.ds(((1 - core) * 4 + z) * 4, 4)], wc_recv.at[z])
        weighted_shifts(1 - core, z)

    fetch(0)

    @pl.loop(0, 4)
    def _(step):
        z = z_in(step)
        weighted_shifts(core, z)

        @pl.when(step < 3)
        def _():
            fetch(step + 1)

        other_half(z)

        @pl.when(step < 3)
        def _():
            q0_ref[...] += jnp.dot(a2_ref[z], t2_ref[...], preferred_element_type=F32)
            q1_ref[...] += jnp.dot(a2_ref[z, :, :256], t2_ref[256:, :], preferred_element_type=F32)

    @pl.loop(0, 2)
    def _(part):
        z = z_in(3)
        to_half = (ms // 4 + 1 + part) % 2
        rows = pl.ds(pl.multiple_of(256 * to_half, 256), 256)
        q0_ref[rows, :] += jnp.dot(a2_ref[z, rows, :], t2_ref[...], preferred_element_type=F32)
        q1_ref[rows, :] += jnp.dot(a2_ref[z, rows, :256], t2_ref[256:, :], preferred_element_type=F32)

        @pl.loop(0, 4)
        def _(turn):
            k = jnp.where(turn == 0, 2, jnp.where(turn == 1, 1, jnp.where(turn == 2, 3, 0)))
            r = (ms + k) % 4
            slot = to_half * 4 + r
            for v in range(6):
                lo, hi = folded(earlier, q0_ref, q1_ref, pl.multiple_of(256 * to_half + 8 * r, 8), 32, v)
                both = jnp.concatenate([lo, hi], 0)
                gf[:, 128 * v : 128 * v + 128] = both
                gmsg[slot, :, 128 * v : 128 * v + 128] = both.astype(BF16)

            @pl.when((part == 0) | (turn < 3))
            def _():
                send(gmsg.at[slot], grecv.at[ms], g_send.at[slot], g_recv.at[ms], sensor_at(slot))

    total = gf[...]
    for k in (1, 3, 2):
        at = (ms // 4) * 4 + (ms + k) % 4
        arrive(grecv.at[at], g_recv.at[at])
        total = total + grecv[at].astype(F32)
    for k in range(4):
        at = (1 - ms // 4) * 4 + (ms + k) % 4
        arrive(grecv.at[at], g_recv.at[at])
        total = total + grecv[at].astype(F32)
    for v in range(6):
        for t in range(2):
            out_ref[8 * v : 8 * v + 8, 128 * t : 128 * t + 128] = total[8 * t : 8 * t + 8, 128 * v : 128 * v + 128]

    for copy in sent:
        copy.wait_send()
    for k in range(1, 8):
        slot = (ms + k) % 8
        sent_off(gmsg.at[slot], g_send.at[slot])

    @pl.loop(0, 4)
    def _(b):
        sent_off(ybuf.at[b, 0], c_send.at[b])
        sent_off(wall.at[pl.ds((core * 4 + b) * 4, 4)], wc_send.at[b])
        for dy in range(4):

            @pl.when((b < 3) | (dy > 0))
            def _():
                sent_off(ybuf.at[b, 1, (y + dy) % 4], z_send.at[b, dy])


def shards(histories, kernel, noise_weight):
    V, S = pltpu.VMEM, pltpu.SemaphoreType.DMA
    out = pl.pallas_call(
        body,
        out_shape=jax.ShapeDtypeStruct((48, 256), F32),
        in_specs=[pl.BlockSpec(memory_space=pltpu.HBM)] * 3,
        out_specs=pl.BlockSpec(memory_space=pltpu.VMEM),
        scratch_shapes=[
            V((64, 64, 256), BF16), V((64, 256), F32), V((2, 4608, 128), F32), V((2, 512, 1024), BF16),
            V((1024, 1024), BF16), V((4, 128, 2048), BF16), V((4, 512, 512), BF16), V((2048, 768), BF16),
            V((128, 768), F32), V((128, 768), F32), V((512, 768), BF16), V((512, 768), F32), V((512, 768), F32),
            V((8, 48, 256), BF16), V((4, 2, 4, 8, 384), F32), V((4, 4, 8, 384), F32), V((16, 8, 384), F32),
            V((32, 16, 256), BF16), V((16, 768), F32), V((8, 16, 768), BF16), V((8, 16, 768), BF16),
            S((6,)), pltpu.SemaphoreType.REGULAR((2,)), S((8,)), S((8,)), S((4,)), S((4,)), S((4, 4)), S((16,)), S((16,)), S((16,)), S((4,)), S((4,)),
            S((8,)), S((8,)),
        ],
        compiler_params=pltpu.CompilerParams(
            collective_id=0, has_side_effects=True, vmem_limit_bytes=60 * 2**20
        ),
        cost_estimate=pl.CostEstimate(flops=4831838208, bytes_accessed=2300000, transcendentals=0),
        name="hessian",
    )(kernel, histories.transpose(1, 0, 2).reshape(48, 256), noise_weight)
    return out.reshape(6, 8, 256).transpose(1, 0, 2)


def solution(mesh):
    in_specs = (P(("param", "sensor"), None, None), P("sensor", "param", None), P("sensor", None))
    out_specs = P(("param", "sensor"), None, None)
    return jax.shard_map(shards, mesh=mesh, in_specs=in_specs, out_specs=out_specs, check_vma=False)
```
